32 devices in a mesh: section: 2 (over core), ctx: 4 (over z), hd: 4 (over y, x).
Axes of the slice: x: 2, y: 2, z: 4, core: 2. Of those that a mesh axis runs over, the one named last changes fastest.
Arguments:
- tokens_in: bfloat16 [2, 1024, 768], P(None, ('ctx', 'hd')), may hold values from -6 to 6
- grad_out: bfloat16 [2, 1024, 768], P(None, ('ctx', 'hd')), may hold values from -6 to 6
- w_query: bfloat16 [2, 768, 768], P('section', ('ctx', 'hd')), may hold values from -0.21875 to 0.21875
- w_key: bfloat16 [2, 768, 768], P('section', ('ctx', 'hd')), may hold values from -0.21875 to 0.21875
- w_value: bfloat16 [2, 768, 768], P('section', ('ctx', 'hd')), may hold values from -0.21875 to 0.21875
- w_output: bfloat16 [2, 768, 768], P('section', ('ctx', 'hd')), may hold values from -1.25 to 1.25
- gain_attn: bfloat16 [2, 768], P('section', ('ctx', 'hd')), may hold values from 0.5 to 1.5
- gain_ffn: bfloat16 [2, 768], P('section', ('ctx', 'hd')), may hold values from 0.5 to 1.5
- router: bfloat16 [2, 768, 4], P('section', ('ctx', 'hd')), may hold values from -0.15625 to 0.15625
- rel_bias: bfloat16 [2, 384], P('section', ('ctx', 'hd')), may hold values from -4 to 4
- w_in: bfloat16 [2, 4, 768, 3072], P('section', 'ctx', None, 'hd'), may hold values from -0.21875 to 0.21875
- w_out: bfloat16 [2, 4, 3072, 768], P('section', 'ctx', 'hd'), may hold values from -0.4375 to 0.4375
- routes: int32 [2, 2, 1024, 1], P('section', None, ('ctx', 'hd')), may hold values from 0 to 3; in each aligned block of 64 rows (0 to 63, 64 to 127, ..., all dimensions but the last counted through in order) at most 32 rows name the same one
- relative_bucket: int32 [511], replicated, may hold values from 0 to 31
Outputs:
- section_out: bfloat16 [2, 2, 1024, 768], P('section', None, ('ctx', 'hd'))
- in_grad: bfloat16 [2, 2, 1024, 768], P('section', None, ('ctx', 'hd'))
- g_query: float32 [2, 768, 768], P('section', ('ctx', 'hd'))
- g_key: float32 [2, 768, 768], P('section', ('ctx', 'hd'))
- g_value: float32 [2, 768, 768], P('section', ('ctx', 'hd'))
- g_output: float32 [2, 768, 768], P('section', ('ctx', 'hd'))
- g_gain_attn: float32 [2, 768], P('section', ('ctx', 'hd'))
- g_gain_ffn: float32 [2, 768], P('section', ('ctx', 'hd'))
- g_router: float32 [2, 768, 4], P('section', ('ctx', 'hd'))
- g_rel_bias: float32 [2, 384], P('section', ('ctx', 'hd'))
- g_w_in: float32 [2, 4, 768, 3072], P('section', 'ctx', None, 'hd')
- g_w_out: float32 [2, 4, 3072, 768], P('section', 'ctx', 'hd')
The draws below stay inside these ranges and needn't reach their ends.
Inputs may be any that keep to these rules, and one draw needn't show every extreme that they name: `routes`: in each aligned block of 64 rows (one device's tokens of one micro-batch and section) no expert is named by more than 32 tokens, a bound that some block reaches.
All inputs are finite; a program needn't handle non-finite values.
Results may differ from the reference program's by a relative error of at most 0.025.
Values may be sent and summed in bfloat16 or wider, within the bound.
A program may use at most 192 MiB of HBM per device.

```python
import math
import jax
import jax.numpy as jnp
import numpy as np
from jax import lax

D = 768
H = 12
HD = 64
FF = 3072
NB = 32
TOK_DEV = 64
MB = 2
SECTIONS = 2
SEQS = 4
SEQ = 256
ROWS = 1024
EXPERTS = 4
CAP = 32


def place_ends(array, key, smallest, high):
    extent = array.shape
    index_at = [jax.random.randint(jax.random.fold_in(key, axis), (), 0, extent[axis]) for axis in range(len(extent))]
    array = array.at[tuple(index_at)].set(smallest)
    longest = extent.index(max(extent))
    index_at[longest] = (index_at[longest] + 1) % extent[longest]
    return array.at[tuple(index_at)].set(high)


def block_levels(rng, extent, shards, low, top_value):
    level, own = 1.0, jax.random.fold_in(rng, 6)
    for axis_at, parts in shards:
        draws = jnp.exp(jax.random.uniform(jax.random.fold_in(own, axis_at), (parts,), jnp.float32, low / len(shards), top_value / len(shards)))
        level = level * jnp.repeat(draws, extent[axis_at] // parts).reshape([-1 if axis == axis_at else 1 for axis in range(len(extent))])
    return level


def shared_out(rng, own, number, rows, amount, top, bound, slope):
    sequence = jax.random.permutation(rng, amount)
    heavy_load, usual = shares(amount, rows * top, bound, slope, True), shares(amount, rows * top, bound, slope, False)
    places = jnp.arange(amount)

    def named(tallies, turn):
        used = int((tallies > 0).sum())
        fixed = max(1, used // 4)
        shifted = fixed + (places - fixed + turn * (used - fixed)) % max(1, amount - fixed)
        return jnp.zeros((amount,), jnp.int32).at[sequence[jnp.where(places < fixed, places, shifted)]].set(jnp.asarray(tallies, jnp.int32))

    tallies = jnp.where(number % 4 == 0, named(heavy_load, number // 4), named(usual, number - number // 4 - 1))
    mixed = jax.random.permutation(jax.random.fold_in(own, 3), amount)
    giver, taker = mixed[0:amount // 2 * 2:2], mixed[1:amount // 2 * 2:2]
    slack = jnp.minimum(tallies[giver] - 1, bound - tallies[taker]) // 2
    slack = jnp.where((giver == sequence[0]) | (taker == sequence[0]) | (tallies[taker] == 0), 0, jnp.maximum(slack, 0))
    shifted = jax.random.randint(jax.random.fold_in(own, 4), (amount // 2,), 0, 1 << 20) % (slack + 1)
    tallies = tallies.at[giver].add(-shifted).at[taker].add(shifted)
    members = jnp.searchsorted(jnp.cumsum(tallies), jnp.arange(rows * top), side="right").astype(jnp.int32)
    grid = members.reshape(top, rows).T
    grid = grid[jax.random.permutation(jax.random.fold_in(own, 1), rows)]
    turn = jax.random.randint(jax.random.fold_in(own, 2), (rows, 1), 0, top)
    return jnp.take_along_axis(grid, (jnp.arange(top)[None, :] + turn) % top, axis=1)


def shares(number_of, total, limit, lean, full):
    portions = [(1 << 20) // math.isqrt(rank ** lean) + 1 for rank in range(1, number_of + 1)]
    largest = limit if full else min(limit, max(-(-total // number_of), total * portions[0] // sum(portions)))
    least = 1 if total - largest >= number_of - 1 else 0
    given, surplus = [largest] + [least] * (number_of - 1), total - largest - least * (number_of - 1)
    while surplus > 0:
        candidates = [i for i in range(1, number_of) if given[i] < largest] or [i for i in range(1, number_of) if given[i] < limit]
        mass, remaining = sum([portions[i] for i in candidates]), surplus
        for i in candidates:
            extra = min(limit - given[i], max(1, remaining * portions[i] // mass), surplus)
            given[i] = given[i] + extra
            surplus = surplus - extra
    return np.array(given)


def gaussian(key, shape, spread, limit, pieces=(), kind=jnp.bfloat16):
    level = block_levels(key, shape, pieces, -0.22, 0.18) if pieces else 1.0
    array = jax.random.normal(key, shape, jnp.float32) * spread * level
    return jnp.minimum(jnp.maximum(array, -limit), limit).astype(kind)


def setup_inputs(seed: int = 0) -> dict:
    splits = jax.random.split(jax.random.key(seed), 15)
    tokens_in = gaussian(splits[0], (MB, ROWS, D), 1.0, 6.0, ((1, 16),))
    grad_out = gaussian(splits[1], (MB, ROWS, D), 1.0, 6.0, ((1, 16),))
    w_query = gaussian(splits[2], (SECTIONS, D, D), D ** -0.5, 0.21875, ((0, 2), (1, 16)))
    w_key = gaussian(splits[3], (SECTIONS, D, D), D ** -0.5, 0.21875, ((0, 2), (1, 16)))
    w_value = gaussian(splits[4], (SECTIONS, D, D), D ** -0.5, 0.21875, ((0, 2), (1, 16)))
    w_output = gaussian(splits[5], (SECTIONS, D, D), (max(1, D * 8 // SEQ)) ** -0.5, 1.25, ((0, 2), (1, 16)))
    gain_attn = jnp.clip(1.0 + 0.1 * jax.random.normal(splits[6], (SECTIONS, D), jnp.float32), 0.5, 1.5).astype(jnp.bfloat16)
    gain_ffn = jnp.clip(1.0 + 0.1 * jax.random.normal(splits[7], (SECTIONS, D), jnp.float32), 0.5, 1.5).astype(jnp.bfloat16)
    router = gaussian(splits[8], (SECTIONS, D, EXPERTS), (2 * D) ** -0.5, 0.15625, ((0, 2), (1, 16)))
    rel_bias = gaussian(splits[9], (SECTIONS, H * NB), 1.0, 4.0, ((0, 2), (1, 16)))
    w_in = gaussian(splits[10], (SECTIONS, EXPERTS, D, FF), D ** -0.5, 0.21875, ((0, 2), (1, 4), (3, 4)))
    w_out = gaussian(splits[11], (SECTIONS, EXPERTS, FF, D), (max(1, FF // (EXPERTS * EXPERTS))) ** -0.5, 0.4375, ((0, 2), (1, 4), (2, 4)))
    routes_keys = jax.random.split(jax.random.fold_in(splits[12], 1), SECTIONS * MB * ROWS // TOK_DEV)
    routes_turns = jax.random.permutation(jax.random.fold_in(splits[12], 3), SECTIONS * MB * ROWS // TOK_DEV)
    routes = jax.vmap(lambda own, number: shared_out(jax.random.fold_in(splits[12], 2), own, number, TOK_DEV, EXPERTS, 1, CAP, 1))(routes_keys, routes_turns).reshape((SECTIONS, MB, ROWS, 1))
    relative_bucket = place_ends(jax.random.randint(splits[13], (2 * SEQ - 1,), 0, NB), jax.random.fold_in(splits[13], 1), 0, NB - 1).astype(jnp.int32)
    return {"tokens_in": tokens_in, "grad_out": grad_out, "w_query": w_query, "w_key": w_key, "w_value": w_value, "w_output": w_output, "gain_attn": gain_attn, "gain_ffn": gain_ffn, "router": router, "rel_bias": rel_bias, "w_in": w_in, "w_out": w_out, "routes": routes, "relative_bucket": relative_bucket}


epsilon = 1e-06
highest = lax.Precision.HIGHEST

@jax.custom_vjp
def low(v):
    return lax.optimization_barrier(v.astype(jnp.bfloat16)).astype(jnp.float32)

@jax.custom_vjp
def low_back(v):
    return v

def low_keep(v):
    return (low(v), None)

def low_pass(kept, grad):
    return (grad,)

def back_keep(v):
    return (v, None)

def back_low(kept, grad):
    return (low(grad),)
low.defvjp(low_keep, low_pass)
low_back.defvjp(back_keep, back_low)

def rms_norm(hidden, gain):
    return hidden * lax.rsqrt(lax.optimization_barrier(jnp.mean(hidden * hidden, axis=-1, keepdims=True)) + epsilon) * gain

def to_sequences(rows):
    return rows.reshape(SEQ // TOK_DEV, SEQS, TOK_DEV, H, HD).transpose(1, 0, 2, 3, 4).reshape(SEQS, SEQ, H, HD)

def from_sequences(values):
    return values.reshape(SEQS, SEQ // TOK_DEV, TOK_DEV, H * HD).transpose(1, 0, 2, 3).reshape(ROWS, H * HD)

def attend(queries, key_rows, value_rows, bias_table, relative_bucket):
    length = queries.shape[0]
    block_rows = min(512, length)
    key_pos = jnp.arange(length, dtype=jnp.int32)

    def one_block(item):
        query_block, offset = item
        query_pos = offset + jnp.arange(block_rows, dtype=jnp.int32)
        bucket_ids = jnp.take(relative_bucket, query_pos[:, None] - key_pos[None, :] + (length - 1))
        scores = jnp.einsum('qhd,khd->hqk', query_block, key_rows, precision=highest) * HD ** (-0.5)
        scores = low_back(scores + jnp.take(bias_table, bucket_ids, axis=1))
        weights = low(jax.nn.softmax(scores, axis=-1))
        return jnp.einsum('hqk,khd->qhd', weights, value_rows, precision=highest)
    query_blocks = queries.reshape(length // block_rows, block_rows, H, HD)
    offsets = block_rows * jnp.arange(length // block_rows, dtype=jnp.int32)
    return lax.map(jax.checkpoint(one_block), (query_blocks, offsets)).reshape(length, H * HD)

def experts(normed, route_ids, router, w_in, w_out):
    router_probs = jax.nn.softmax(jnp.dot(normed, router, precision=highest), axis=-1)
    chosen = route_ids[:, None] == jnp.arange(EXPERTS, dtype=jnp.int32)[None, :]
    gate_value = lax.optimization_barrier(jnp.sum(jnp.where(chosen, router_probs, 0.0), axis=-1))
    chosen_int = chosen.astype(jnp.int32)
    slot_rank = lax.optimization_barrier(jnp.sum((jnp.cumsum(chosen_int, axis=0) - chosen_int) * chosen_int, axis=-1))
    dispatched = low_back(normed)
    slot_rows = jnp.zeros((EXPERTS, ROWS // TOK_DEV * CAP, D), jnp.float32).at[route_ids, slot_rank].set(dispatched)
    hidden = low_back(jnp.einsum('esd,edf->esf', slot_rows, w_in, precision=highest))
    active = low(jax.nn.gelu(hidden))
    result = low(low_back(jnp.einsum('esf,efd->esd', active, w_out, precision=highest)))
    return gate_value[:, None] * result[route_ids, slot_rank]

def section_layer(section_in, w_query, w_key, w_value, w_output, gain_attn, gain_ffn, router, bias_table, w_in, w_out, route_ids, relative_bucket):
    section_rows = []
    for micro_batch in range(MB):
        resid_in = low_back(section_in[micro_batch])
        normed = low(rms_norm(resid_in, gain_attn))
        queries = low(low_back(jnp.dot(normed, w_query, precision=highest)))
        key_rows = low(low_back(jnp.dot(normed, w_key, precision=highest)))
        value_rows = low(low_back(jnp.dot(normed, w_value, precision=highest)))

        def one_sequence(trio):
            return attend(trio[0], trio[1], trio[2], bias_table, relative_bucket)
        attended_seq = lax.map(one_sequence, (to_sequences(queries), to_sequences(key_rows), to_sequences(value_rows)))
        attended = low(low_back(from_sequences(attended_seq)))
        resid_mid = resid_in + jnp.dot(attended, w_output, precision=highest)
        normed_two = low(rms_norm(resid_mid, gain_ffn))
        section_rows.append(low(resid_mid + experts(normed_two, route_ids[micro_batch], router, w_in, w_out)))
    return jnp.stack(section_rows)

def reference(tokens_in, grad_out, w_query, w_key, w_value, w_output, gain_attn, gain_ffn, router, rel_bias, w_in, w_out, routes, relative_bucket):

    def section_params(section_index):
        dense_list = tuple((weight[section_index].astype(jnp.float32) for weight in (w_query, w_key, w_value, w_output, gain_attn, gain_ffn, router)))
        return dense_list + (rel_bias[section_index].astype(jnp.float32).reshape(H, NB), w_in[section_index].astype(jnp.float32), w_out[section_index].astype(jnp.float32))

    def section_fn(section_index):

        def apply_layer(section_in, *weight_list):
            return section_layer(section_in, *weight_list, routes[section_index, :, :, 0], relative_bucket)
        return apply_layer
    first_out, back_first = jax.vjp(section_fn(0), tokens_in.astype(jnp.float32), *section_params(0))
    second_out, back_second = jax.vjp(section_fn(1), first_out, *section_params(1))
    grads_second = back_second(grad_out.astype(jnp.float32))
    grads_first = back_first(grads_second[0])

    def stacked_grad(token_position):
        return jnp.stack([grads_first[token_position], grads_second[token_position]])
    return (jnp.stack([first_out, second_out]).astype(jnp.bfloat16), stacked_grad(0).astype(jnp.bfloat16), stacked_grad(1), stacked_grad(2), stacked_grad(3), stacked_grad(4), stacked_grad(5), stacked_grad(6), stacked_grad(7), stacked_grad(8).reshape(SECTIONS, H * NB), stacked_grad(9), stacked_grad(10))
```

```python
import functools
import math

import jax
import jax.numpy as jnp
from jax import lax
from jax.experimental import pallas as pl
from jax.experimental.pallas import tpu as pltpu
from jax.sharding import PartitionSpec as P

H = 12
HD = 64
MB = 2


epsilon = 1e-06
highest = lax.Precision.HIGHEST


def from_behind(value, axis, steps):
    count = lax.axis_size(axis)
    first, last = (max(0, -steps), min(count, count - steps))
    return lax.ppermute(value, axis, [(source, source + steps) for source in range(first, last)])


def split_up(value, dim, size):
    shape = value.shape
    tiles = value.reshape(*shape[:dim], size, shape[dim] // size, *shape[dim + 1 :])
    return jnp.moveaxis(tiles, dim, 0)


def summed_on_arrival(value, axis, dim):
    size = lax.axis_size(axis)
    tiles = lax.all_to_all(split_up(value, dim, size), axis, 0, 0, tiled=True)
    return jnp.sum(tiles.astype(jnp.float32), axis=0)


def in_one_piece(arrays, axis, dim, along):
    columns = [a.reshape(*a.shape[:along], -1) for a in arrays]
    both = jnp.concatenate(columns, axis=along)
    out, at, outs = (summed_on_arrival(both, axis, dim), 0, [])
    for a, column in zip(arrays, columns):
        section = out[..., at : at + column.shape[along]]
        outs.append(section.reshape(*section.shape[:along], *a.shape[along:]))
        at += column.shape[along]
    return tuple(outs)


def rms_norm(hidden, gain):
    return hidden * lax.rsqrt(jnp.mean(hidden * hidden, axis=-1, keepdims=True) + epsilon) * gain


def over_blocks(update, running, stacked_arrays):
    row_span = stacked_arrays.shape[2]
    block_rows = math.gcd(row_span, 512)

    def advance(inner_state, block_index):
        first_row = block_index * block_rows
        portion = lax.dynamic_slice_in_dim(stacked_arrays, first_row, block_rows, 2)
        return (update(inner_state, portion, first_row), None)

    running, _ = lax.scan(advance, running, jnp.arange(row_span // block_rows, dtype=jnp.int32))
    return running


def bucket_lookup(relative_bucket, query_pos, key_pos):
    length = (relative_bucket.shape[0] + 1) // 2
    return jnp.take(relative_bucket, query_pos[:, None] - key_pos[None, :] + (length - 1))


def scores_of(queries, key_block, bias_table, bucket_ids):
    raw = jnp.einsum("sqhd,skhd->shqk", queries, key_block, preferred_element_type=jnp.float32)
    return raw * queries.shape[-1] ** (-0.5) + jnp.take(bias_table, bucket_ids, axis=1)[None]


def score_grads(
    queries, grad_heads, logsumexp_total, row_delta, key_block, value_block, bias_table, bucket_ids
):
    scores = scores_of(queries, key_block, bias_table, bucket_ids)
    weights = jnp.exp(scores - logsumexp_total[..., None])
    grad_weights = jnp.einsum(
        "sqhd,skhd->shqk", grad_heads, value_block, preferred_element_type=jnp.float32
    )
    score_gradient = (weights * (grad_weights - row_delta[..., None])).astype(jnp.bfloat16)
    return (score_gradient, weights.astype(jnp.bfloat16))


def bias_grad(score_gradient, bucket_ids, bucket_count):
    marker_flags = (
        bucket_ids[None] == jnp.arange(bucket_count, dtype=jnp.int32)[:, None, None]
    ).astype(jnp.bfloat16)
    return jnp.einsum(
        "shqk,mqk->hm", score_gradient, marker_flags, preferred_element_type=jnp.float32
    )


def to_heads(stacked_arrays):
    return lax.all_to_all(stacked_arrays, "hd", split_axis=3, concat_axis=1, tiled=True)


def to_rows(stacked_arrays):
    return lax.all_to_all(stacked_arrays, "hd", split_axis=1, concat_axis=3, tiled=True)


def cycle_fold(stacked_arrays, update, running):
    return over_blocks(update, running, lax.all_gather(stacked_arrays, "ctx", axis=2, tiled=True))


def expert_swap(slots):
    return lax.all_to_all(slots, "ctx", split_axis=0, concat_axis=0, tiled=True)


def expert_gather(slots):
    return lax.all_gather(slots, "hd", axis=0, tiled=True)


def expert_sum(term, row_total):
    return lax.psum_scatter(
        term(jnp.int32(0), row_total * lax.axis_size("hd")).astype(jnp.bfloat16),
        "hd",
        scatter_dimension=0,
        tiled=True,
    ).astype(jnp.float32)


def on_device(
    tokens_in,
    grad_out,
    w_query,
    w_key,
    w_value,
    w_output,
    gain_attn,
    gain_ffn,
    router,
    rel_bias,
    w_in,
    w_out,
    routes,
    relative_bucket,
):
    is_first = lax.axis_index("section") == 0
    hd_count = lax.axis_size("hd")
    head_group = H // hd_count
    gathered_weights = (
        lax.all_gather(w_query, ("ctx", "hd"), axis=1, tiled=True),
        lax.all_gather(w_key, ("ctx", "hd"), axis=1, tiled=True),
        lax.all_gather(w_value, ("ctx", "hd"), axis=1, tiled=True),
        lax.all_gather(w_output, ("ctx", "hd"), axis=1, tiled=True),
        lax.all_gather(gain_attn, ("ctx", "hd"), axis=1, tiled=True),
        lax.all_gather(gain_ffn, ("ctx", "hd"), axis=1, tiled=True),
        lax.all_gather(router, ("ctx", "hd"), axis=1, tiled=True),
        lax.all_gather(rel_bias, ("ctx", "hd"), axis=1, tiled=True),
    )
    w_stack = jnp.stack([gathered_weights[0][0], gathered_weights[1][0], gathered_weights[2][0]])
    w_mix = gathered_weights[3][0]
    gain_first = gathered_weights[4][0].astype(jnp.float32)
    gain_second = gathered_weights[5][0].astype(jnp.float32)
    w_route = gathered_weights[6][0]
    bucket_count = gathered_weights[7].shape[1] // H
    all_bias = gathered_weights[7][0].astype(jnp.float32).reshape(H, bucket_count)
    bias_table = lax.dynamic_slice_in_dim(
        all_bias, lax.axis_index("hd") * head_group, head_group, 0
    )
    expert_in = w_in[0, 0]
    expert_out = w_out[0, 0]
    row_count = tokens_in.shape[1]
    query_pos = lax.axis_index("ctx") * row_count + jnp.arange(row_count, dtype=jnp.int32)
    expert_count = router.shape[2]
    capacity = max(2, 2 * row_count // expert_count)
    slot_total = expert_count * capacity
    length = (relative_bucket.shape[0] + 1) // 2
    scale = HD ** (-0.5)
    group_width = head_group * HD
    contract_rows = (((0,), (0,)), ((), ()))
    contract_cols = (((1,), (1,)), ((), ()))

    def backward(saved, cotangent):
        (
            resid_in,
            normed,
            grouped,
            logsumexp_total,
            attended_full,
            attended,
            resid_mid,
            normed_two,
            router_probs,
            gate_value,
            chosen,
            dispatch,
            routed_rows,
            hidden,
            active,
            combined,
        ) = saved
        grad_gate = jnp.sum(cotangent * combined, axis=-1)
        grad_logits = router_probs * (
            jnp.where(chosen, grad_gate[:, None], 0.0) - (gate_value * grad_gate)[:, None]
        )
        grad_router = lax.dot_general(
            normed_two.astype(jnp.float32), grad_logits, contract_rows, precision=highest
        )
        grad_normed = lax.dot_general(
            grad_logits, w_route.astype(jnp.float32), contract_cols, precision=highest
        )
        grad_slots = jnp.dot(
            dispatch.astype(jnp.float32), gate_value[:, None] * cotangent, precision=highest
        ).astype(jnp.bfloat16)
        grad_arrived = expert_swap(grad_slots.reshape(expert_count, capacity, -1))
        grad_result = expert_gather(grad_arrived).reshape(-1, cotangent.shape[1])
        grad_active = lax.dot_general(
            grad_result, expert_out, contract_cols, preferred_element_type=jnp.float32
        )
        gelu_back = jax.vjp(jax.nn.gelu, hidden)[1]
        grad_hidden = gelu_back(grad_active)[0].astype(jnp.bfloat16)
        grad_expert_out = lax.dot_general(
            active, grad_result, contract_rows, preferred_element_type=jnp.float32
        )
        grad_expert_in = lax.dot_general(
            routed_rows, grad_hidden, contract_rows, preferred_element_type=jnp.float32
        )

        def in_term(offset, row_span):
            return lax.dot_general(
                grad_hidden, expert_in, contract_cols, preferred_element_type=jnp.float32
            )

        grad_routed = expert_sum(in_term, grad_arrived.shape[0] * capacity).astype(jnp.bfloat16)
        grad_returned = expert_swap(
            grad_routed.reshape(-1, capacity, grad_routed.shape[1])
        ).reshape(slot_total, -1)
        grad_normed = grad_normed + lax.dot_general(
            dispatch, grad_returned, contract_rows, preferred_element_type=jnp.float32
        )
        norm_back = jax.vjp(rms_norm, resid_mid, gain_second)[1]
        grad_mid, grad_gain_second = norm_back(grad_normed)
        grad_mid = grad_mid + cotangent
        grad_mix = lax.dot_general(
            attended.astype(jnp.float32), grad_mid, contract_rows, precision=highest
        )
        grad_attended = lax.dot_general(
            grad_mid, w_mix.astype(jnp.float32), contract_cols, precision=highest
        ).astype(jnp.bfloat16)
        grad_heads = to_heads(grad_attended[None, None])[0]
        queries = grouped[0].reshape(hd_count, row_count, head_group, HD)
        grad_query_heads = grad_heads.reshape(hd_count, row_count, head_group, HD)
        row_delta = jnp.einsum(
            "sqhd,sqhd->shq", grad_query_heads.astype(jnp.float32), attended_full
        )

        def summed_update(running, portion, offset):
            query_sum, bias_sum, key_sums = running
            key_block = portion[0].reshape(hd_count, -1, head_group, HD)
            value_block = portion[1].reshape(hd_count, -1, head_group, HD)
            span = portion.shape[2]
            bucket_ids = bucket_lookup(
                relative_bucket, query_pos, offset + jnp.arange(span, dtype=jnp.int32)
            )
            score_gradient, weights = score_grads(
                queries,
                grad_query_heads,
                logsumexp_total,
                row_delta,
                key_block,
                value_block,
                bias_table,
                bucket_ids,
            )
            query_sum = query_sum + jnp.einsum(
                "shqk,skhd->sqhd", score_gradient, key_block, preferred_element_type=jnp.float32
            )
            bias_sum = bias_sum + bias_grad(score_gradient, bucket_ids, bucket_count)
            key_part = jnp.einsum(
                "shqk,sqhd->skhd", score_gradient, queries, preferred_element_type=jnp.float32
            )
            value_part = jnp.einsum(
                "shqk,sqhd->skhd", weights, grad_query_heads, preferred_element_type=jnp.float32
            )
            fresh = jnp.stack([key_part, value_part]).reshape(2, hd_count, span, group_width)
            current = lax.dynamic_slice_in_dim(key_sums, offset, span, 2)
            key_sums = lax.dynamic_update_slice_in_dim(key_sums, current + fresh, offset, 2)
            return (query_sum, bias_sum, key_sums)

        start_grads = (
            jnp.zeros((hd_count, row_count, head_group, HD), jnp.float32),
            jnp.zeros((head_group, bucket_count), jnp.float32),
            jnp.zeros((2, hd_count, length, group_width), jnp.float32),
        )
        query_sum, bias_sum, key_sums = cycle_fold(grouped[1:3], summed_update, start_grads)
        key_grads = lax.psum_scatter(
            key_sums.astype(jnp.bfloat16), "ctx", scatter_dimension=2, tiled=True
        ).astype(jnp.float32)
        grad_qkv = jnp.stack(
            [
                (query_sum * scale).reshape(hd_count, row_count, group_width),
                key_grads[0] * scale,
                key_grads[1],
            ]
        ).astype(jnp.bfloat16)
        grad_rows = to_rows(grad_qkv)[:, 0]
        grad_stack = jnp.einsum(
            "rd,sre->sde", normed, grad_rows, preferred_element_type=jnp.float32
        )
        grad_normed_one = jnp.einsum(
            "sre,sde->rd", grad_rows, w_stack, preferred_element_type=jnp.float32
        )
        norm_back_one = jax.vjp(rms_norm, resid_in, gain_first)[1]
        grad_input, grad_gain_first = norm_back_one(grad_normed_one)
        grad_input = (grad_input + grad_mid).astype(jnp.bfloat16)
        return (
            grad_input,
            (
                grad_stack,
                grad_mix,
                grad_gain_first,
                grad_gain_second,
                grad_router,
                bias_sum,
                grad_expert_in,
                grad_expert_out,
            ),
        )

    received = jnp.zeros((row_count, tokens_in.shape[2]), jnp.bfloat16)
    saved_list = []
    produced_list = []
    for tick_index in range(MB + 1):
        section_input = jnp.where(is_first, tokens_in[min(tick_index, MB - 1)], received)
        route_ids = jnp.where(
            is_first,
            routes[0, min(tick_index, MB - 1), :, 0],
            routes[0, max(tick_index - 1, 0), :, 0],
        )
        forward_resid_in = section_input.astype(jnp.float32)
        forward_normed = rms_norm(forward_resid_in, gain_first).astype(jnp.bfloat16)
        projected = jnp.einsum(
            "rd,sde->sre", forward_normed, w_stack, preferred_element_type=jnp.float32
        ).astype(jnp.bfloat16)
        forward_grouped = to_heads(projected[:, None])
        forward_queries = forward_grouped[0].reshape(hd_count, row_count, head_group, HD)

        def stats_update(running, portion, offset):
            row_max, row_sum = running
            key_pos = offset + jnp.arange(portion.shape[2], dtype=jnp.int32)
            scores = scores_of(
                forward_queries,
                portion[0].reshape(hd_count, -1, head_group, HD),
                bias_table,
                bucket_lookup(relative_bucket, query_pos, key_pos),
            )
            new_max = jnp.maximum(row_max, jnp.max(scores, axis=-1))
            row_sum = row_sum * jnp.exp(row_max - new_max) + jnp.sum(
                jnp.exp(scores - new_max[..., None]), axis=-1
            )
            return (new_max, row_sum)

        start_stats = (
            jnp.full((hd_count, head_group, row_count), -1e30, jnp.float32),
            jnp.zeros((hd_count, head_group, row_count), jnp.float32),
        )
        row_max, row_sum = cycle_fold(forward_grouped[1:2], stats_update, start_stats)
        forward_logsumexp_total = row_max + jnp.log(row_sum)

        def value_update(running, portion, offset):
            key_pos = offset + jnp.arange(portion.shape[2], dtype=jnp.int32)
            scores = scores_of(
                forward_queries,
                portion[0].reshape(hd_count, -1, head_group, HD),
                bias_table,
                bucket_lookup(relative_bucket, query_pos, key_pos),
            )
            weights = jnp.exp(scores - forward_logsumexp_total[..., None]).astype(jnp.bfloat16)
            return running + jnp.einsum(
                "shqk,skhd->sqhd",
                weights,
                portion[1].reshape(hd_count, -1, head_group, HD),
                preferred_element_type=jnp.float32,
            )

        forward_attended_full = cycle_fold(
            forward_grouped[1:3],
            value_update,
            jnp.zeros((hd_count, row_count, head_group, HD), jnp.float32),
        )
        forward_attended = to_rows(
            forward_attended_full.reshape(1, hd_count, row_count, group_width).astype(jnp.bfloat16)
        )[0, 0]
        forward_resid_mid = forward_resid_in + jnp.dot(
            forward_attended, w_mix, preferred_element_type=jnp.float32
        )
        forward_normed_two = rms_norm(forward_resid_mid, gain_second).astype(jnp.bfloat16)
        forward_router_probs = jax.nn.softmax(
            jnp.dot(forward_normed_two, w_route, preferred_element_type=jnp.float32), axis=-1
        )
        forward_chosen = route_ids[:, None] == jnp.arange(expert_count, dtype=jnp.int32)[None, :]
        forward_gate_value = jnp.sum(jnp.where(forward_chosen, forward_router_probs, 0.0), axis=-1)
        chosen_int = forward_chosen.astype(jnp.int32)
        slot_rank = jnp.sum((jnp.cumsum(chosen_int, axis=0) - chosen_int) * chosen_int, axis=-1)
        slot_index = route_ids * capacity + slot_rank
        forward_dispatch = (
            jnp.arange(slot_total, dtype=jnp.int32)[:, None] == slot_index[None, :]
        ).astype(jnp.bfloat16)
        outgoing = jnp.dot(
            forward_dispatch, forward_normed_two, preferred_element_type=jnp.float32
        ).astype(jnp.bfloat16)
        arrived = expert_swap(outgoing.reshape(expert_count, capacity, -1))
        forward_routed_rows = expert_gather(arrived).reshape(-1, forward_normed_two.shape[1])
        forward_hidden = jnp.dot(forward_routed_rows, expert_in, preferred_element_type=jnp.float32)
        forward_active = jax.nn.gelu(forward_hidden).astype(jnp.bfloat16)

        def out_term(offset, row_span):
            return jnp.dot(forward_active, expert_out, preferred_element_type=jnp.float32)

        result = expert_sum(out_term, arrived.shape[0] * capacity).astype(jnp.bfloat16)
        returned = expert_swap(result.reshape(-1, capacity, result.shape[1])).reshape(
            slot_total, -1
        )
        forward_combined = lax.dot_general(
            forward_dispatch, returned, contract_rows, preferred_element_type=jnp.float32
        )
        section_output = (
            forward_resid_mid + forward_gate_value[:, None] * forward_combined
        ).astype(jnp.bfloat16)
        forward_saved = (
            forward_resid_in,
            forward_normed,
            forward_grouped,
            forward_logsumexp_total,
            forward_attended_full,
            forward_attended,
            forward_resid_mid,
            forward_normed_two,
            forward_router_probs,
            forward_gate_value,
            forward_chosen,
            forward_dispatch,
            forward_routed_rows,
            forward_hidden,
            forward_active,
            forward_combined,
        )
        saved = forward_saved
        saved_list.append(saved)
        produced_list.append(section_output)
        if tick_index < MB:
            received = from_behind(section_output, "section", 1)
    incoming = jnp.zeros((row_count, tokens_in.shape[2]), jnp.float32)
    grad_total = None
    grad_list = []
    for tick_index in range(MB + 1):
        last_cot = (
            grad_out[max(MB - 1 - tick_index, 0)].astype(jnp.float32)
            if tick_index < MB
            else jnp.zeros_like(incoming)
        )
        cotangent = jnp.where(is_first, incoming, last_cot)
        grad_input, grad_parts = backward(saved_list[MB - tick_index], cotangent)
        grad_total = (
            grad_parts if grad_total is None else jax.tree.map(jnp.add, grad_total, grad_parts)
        )
        grad_list.append(grad_input)
        if tick_index < MB:
            incoming = from_behind(grad_input, "section", -1).astype(jnp.float32)
    section_rows = jnp.stack(
        [
            jnp.where(is_first, produced_list[micro_index], produced_list[micro_index + 1])
            for micro_index in range(MB)
        ]
    )[None]
    grad_rows_out = jnp.stack(
        [
            jnp.where(is_first, grad_list[MB - micro_index], grad_list[MB - 1 - micro_index])
            for micro_index in range(MB)
        ]
    )[None]
    (
        grad_stack,
        grad_mix,
        grad_gain_first,
        grad_gain_second,
        grad_router,
        bias_sum,
        grad_expert_in,
        grad_expert_out,
    ) = grad_total
    bias_full = lax.dynamic_update_slice_in_dim(
        jnp.zeros((H, bucket_count), jnp.float32), bias_sum, lax.axis_index("hd") * head_group, 0
    )
    summed_grads = (
        *in_one_piece(
            (
                grad_stack[0].astype(jnp.bfloat16),
                grad_stack[1].astype(jnp.bfloat16),
                grad_stack[2].astype(jnp.bfloat16),
                grad_mix.astype(jnp.bfloat16),
                grad_gain_first.astype(jnp.bfloat16),
                grad_gain_second.astype(jnp.bfloat16),
                grad_router.astype(jnp.bfloat16),
            ),
            ("ctx", "hd"),
            0,
            1,
        ),
        summed_on_arrival(bias_full.reshape(-1).astype(jnp.bfloat16), ("ctx", "hd"), 0),
    )
    return (
        section_rows,
        grad_rows_out,
        summed_grads[0][None],
        summed_grads[1][None],
        summed_grads[2][None],
        summed_grads[3][None],
        summed_grads[4][None],
        summed_grads[5][None],
        summed_grads[6][None],
        summed_grads[7][None],
        grad_expert_in[None, None],
        grad_expert_out[None, None],
    )


def gather_over(value, axis):
    return lax.all_gather(value, axis, axis=0, tiled=False)


def exchange(tiles, axis):
    return lax.all_to_all(tiles, axis, split_axis=0, concat_axis=0, tiled=True)


def sum_over(tiles, axis):
    return jnp.sum(exchange(tiles.astype(jnp.bfloat16), axis).astype(jnp.float32), axis=0)


def dot_f32(a, b, dims=(((1,), (0,)), ((), ()))):
    return lax.dot_general(a, b, dims, preferred_element_type=jnp.float32)


ROWS_IN = (((0,), (0,)), ((), ()))
COLS_IN = (((1,), (1,)), ((), ()))


def toeplitz(vec_row, length):
    wide = jnp.broadcast_to(vec_row, (length, 2 * length))
    return pltpu.roll(wide, 0, 1, stride=1, stride_axis=0)[:, :length]


MESH_ID = pl.DeviceIdType.MESH


def greet(axes):
    barrier = pltpu.get_barrier_semaphore()
    total = 0
    for axis in axes:
        me, count = lax.axis_index(axis), lax.axis_size(axis)
        for step in range(1, count):
            peer = lax.rem(me + step, count)
            pl.semaphore_signal(barrier, inc=1, device_id={axis: peer}, device_id_type=MESH_ID)
            total += 1
    pl.semaphore_wait(barrier, total)


def begin(src, dst, sems, phase, axis, spread):
    me, count = lax.axis_index(axis), lax.axis_size(axis)
    copies = []
    for step in range(1, count):
        peer = lax.rem(me + step, count)
        copy = pltpu.make_async_remote_copy(
            src_ref=src.at[peer] if spread else src,
            dst_ref=dst.at[me],
            send_sem=sems.at[phase, 0, step - 1],
            recv_sem=sems.at[phase, 1, step - 1],
            device_id={axis: peer},
            device_id_type=MESH_ID,
        )
        copy.start()
        copies.append(copy)
    if spread:
        dst[pl.ds(me, 1)] = src[pl.ds(me, 1)]
    else:
        dst[pl.ds(me, 1)] = src[...][None]
    return copies


def finish(copies):
    for copy in copies:
        copy.wait()


def store_tiles(ref, value):
    for tile in range(ref.shape[0]):
        ref[tile] = value[tile * ref.shape[1] : (tile + 1) * ref.shape[1]]


def load_rows(ref):
    return ref[...].reshape(ref.shape[0] * ref.shape[1], ref.shape[2])


def sum_tiles(ref):
    total = ref[0].astype(jnp.float32)
    for tile in range(1, ref.shape[0]):
        total = total + ref[tile].astype(jnp.float32)
    return total


def rms_norm_back(hidden, gain, grad):
    inverse = lax.rsqrt(jnp.mean(hidden * hidden, axis=-1, keepdims=True) + epsilon)
    scaled = gain * grad
    mean = jnp.mean(hidden * scaled, axis=-1, keepdims=True)
    gain_grad = jnp.sum(hidden * inverse * grad, axis=0, keepdims=True)
    return inverse * scaled - hidden * (inverse * inverse * inverse * mean), gain_grad


def gelu_parts(u):
    scale = math.sqrt(2.0 / math.pi)
    t = jnp.tanh(scale * (u + 0.044715 * (u * u * u)))
    slope = 0.5 * (1.0 + t) + 0.5 * u * (1.0 - t * t) * scale * (1.0 + 3 * 0.044715 * u * u)
    return 0.5 * u * (1.0 + t), slope


def softmax_parts(qkv, bias_ref, head, heads):
    length = qkv.shape[0]
    width = heads * HD
    at = head * HD
    q = qkv[:, at : at + HD]
    k = qkv[:, width + at : width + at + HD]
    v = qkv[:, 2 * width + at : 2 * width + at + HD]
    scores = dot_f32(q, k, COLS_IN) * HD ** (-0.5) + toeplitz(bias_ref[head : head + 1], length)
    powers = jnp.exp(scores - jnp.max(scores, axis=-1, keepdims=True))
    return q, k, v, powers / jnp.sum(powers, axis=-1, keepdims=True)


def attend(qkv, bias_ref, heads):
    outs = []
    for head in range(heads):
        _, _, v, weights = softmax_parts(qkv, bias_ref, head, heads)
        outs.append(dot_f32(weights.astype(jnp.bfloat16), v))
    return jnp.concatenate(outs, axis=1).astype(jnp.bfloat16)


def attend_back(qkv, grads, bias_ref, diag_ref, heads):
    length = qkv.shape[0]
    rows = lax.broadcasted_iota(jnp.int32, (length, length), 0)
    cols = lax.broadcasted_iota(jnp.int32, (length, length), 1)
    flip = jnp.where(rows + cols == length - 1, 1.0, 0.0).astype(jnp.bfloat16)
    dqs, dks, dvs = [], [], []
    diag_ref[...] = jnp.zeros_like(diag_ref)
    for head in range(heads):
        q, k, v, weights = softmax_parts(qkv, bias_ref, head, heads)
        grad = grads[:, head * HD : (head + 1) * HD]
        grad_weights = dot_f32(grad, v, COLS_IN)
        delta = jnp.sum(weights * grad_weights, axis=-1, keepdims=True)
        score_grad = (weights * (grad_weights - delta)).astype(jnp.bfloat16)
        dqs.append(dot_f32(score_grad, k) * HD ** (-0.5))
        dks.append(dot_f32(score_grad, q, ROWS_IN) * HD ** (-0.5))
        dvs.append(dot_f32(weights.astype(jnp.bfloat16), grad, ROWS_IN))
        flipped = dot_f32(flip, score_grad)
        wide = jnp.concatenate([flipped, jnp.zeros_like(flipped)], axis=1)
        rolled = pltpu.roll(wide, 0, 1, stride=1, stride_axis=0)
        diag_ref[head : head + 1] = jnp.sum(rolled, axis=0, keepdims=True)
    return jnp.concatenate(dqs + dks + dvs, axis=1).astype(jnp.bfloat16)


SAVED = ("normed", "qkv", "attended", "mid", "two", "probs", "gate", "disp", "routed", "hidden", "result")


def layer_kernel(mode, heads, names_in, names_out, names_scratch, *refs):
    r = dict(zip(names_in + names_out + names_scratch, refs))
    sems = r["sems"]
    rows, width = r["x"].shape
    experts = r["small"].shape[0] - 2
    greet(("ctx", "hd"))
    gain_one = r["small"][0:1]
    gain_two = r["small"][1:2]
    low = lambda v: v.astype(jnp.bfloat16)

    if mode != "back":
        copies = begin(r["x"], r["all_x"], sems, 0, "ctx", False)
        resid_in = r["x"][...].astype(jnp.float32)
        finish(copies)
        normed = low(rms_norm(load_rows(r["all_x"]).astype(jnp.float32), gain_one))
        r["normed"][...] = normed
        r["qkv"][...] = low(dot_f32(normed, r["w_qkv"][...]))
        r["attended"][...] = attend(r["qkv"], r["bias"], heads)
        store_tiles(r["mix_out"], low(dot_f32(r["attended"][...], r["w_mix"][...])))
        copies = begin(r["mix_out"], r["mix_in"], sems, 1, "ctx", True)
        route = r["route"][...]
        chosen = jnp.where(
            lax.broadcasted_iota(jnp.int32, (rows, experts), 1) == route, 1.0, 0.0
        )
        earlier = jnp.where(
            lax.broadcasted_iota(jnp.int32, (rows, rows), 0)
            > lax.broadcasted_iota(jnp.int32, (rows, rows), 1),
            1.0,
            0.0,
        )
        ranks = dot_f32(low(earlier), low(chosen))
        rank = jnp.sum(ranks * chosen, axis=-1, keepdims=True).astype(jnp.int32)
        slots = r["slot_out"].shape[0] * r["slot_out"].shape[1]
        slot_at = route * (slots // experts) + rank
        disp = low(
            jnp.where(lax.broadcasted_iota(jnp.int32, (rows, slots), 1) == slot_at, 1.0, 0.0)
        )
        r["disp"][...] = disp
        finish(copies)
        mid = resid_in + sum_tiles(r["mix_in"])
        two = low(rms_norm(mid, gain_two))
        logits = dot_f32(two, low(r["small"][2:]), COLS_IN)
        powers = jnp.exp(logits - jnp.max(logits, axis=-1, keepdims=True))
        probs = powers / jnp.sum(powers, axis=-1, keepdims=True)
        gate = jnp.sum(probs * chosen, axis=-1, keepdims=True)
        r["mid"][...] = mid
        r["two"][...] = two
        r["probs"][...] = probs
        r["gate"][...] = gate
    else:
        resid_in = r["x"][...].astype(jnp.float32)
        mid, two, probs, gate = r["mid"][...], r["two"][...], r["probs"][...], r["gate"][...]
        disp = r["disp"][...]
        route = r["route"][...]
        chosen = jnp.where(
            lax.broadcasted_iota(jnp.int32, (rows, experts), 1) == route, 1.0, 0.0
        )

    if mode != "fwd":
        cotangent = r["cot"][...].astype(jnp.float32)
        grad_rows = low(gate * cotangent)
    payload = {
        "fwd": lambda: two,
        "back": lambda: grad_rows,
        "both": lambda: jnp.concatenate([two, grad_rows], axis=1),
    }[mode]()
    store_tiles(r["slot_out"], low(dot_f32(disp, payload, ROWS_IN)))
    finish(begin(r["slot_out"], r["slot_in"], sems, 2, "ctx", True))
    for tile in range(r["slot_in"].shape[0]):
        span = r["slot_in"].shape[1]
        r["mine"][tile * span : (tile + 1) * span] = r["slot_in"][tile]
    finish(begin(r["mine"], r["gathered"], sems, 3, "hd", False))
    tiles, span = r["gathered"].shape[:2]
    for tile in range(tiles):
        at = slice(tile * span, (tile + 1) * span)
        if mode != "back":
            routed = r["gathered"][tile, :, :width]
            hidden = dot_f32(routed, r["w_in"][...])
            r["routed"][at] = routed
            r["hidden"][at] = hidden
        else:
            hidden = r["hidden"][at]
        active, slope = gelu_parts(hidden)
        active = low(active)
        if mode != "back":
            r["term_out"][tile, :, :width] = low(dot_f32(active, r["w_out"][...]))
        if mode != "fwd":
            r["active"][at] = active
            grad_result = r["gathered"][tile, :, -width:]
            r["grad_result"][at] = grad_result
            grad_hidden = low(slope * dot_f32(grad_result, r["w_out"][...], COLS_IN))
            r["grad_hidden"][at] = grad_hidden
            r["term_out"][tile, :, -width:] = low(dot_f32(grad_hidden, r["w_in"][...], COLS_IN))
    copies = begin(r["term_out"], r["term_in"], sems, 4, "hd", True)
    if mode != "fwd":
        r["g_out"][...] = dot_f32(r["active"][...], r["grad_result"][...], ROWS_IN)
    finish(copies)
    store_tiles(r["back_out"], low(sum_tiles(r["term_in"])))
    copies = begin(r["back_out"], r["back_in"], sems, 5, "ctx", True)
    if mode != "fwd":
        r["g_in"][...] = dot_f32(r["routed"][...], r["grad_hidden"][...], ROWS_IN)
    finish(copies)
    returned = dot_f32(disp, load_rows(r["back_in"]))
    if mode != "back":
        result = returned[:, :width]
        r["result"][...] = result
        r["produced"][...] = low(mid + gate * result)
    else:
        result = r["result"][...]
    if mode == "fwd":
        return

    grad_gate = jnp.sum(cotangent * result, axis=-1, keepdims=True)
    grad_logits = probs * (chosen - gate) * grad_gate
    grad_two = returned[:, -width:]
    for expert in range(experts):
        grad_two = grad_two + grad_logits[:, expert : expert + 1] * r["small"][2 + expert : 3 + expert]
    grad_mid, grad_gain_two = rms_norm_back(mid, gain_two, grad_two)
    grad_mid = grad_mid + cotangent
    r["mid_out"][...] = low(grad_mid)
    copies = begin(r["mid_out"], r["mid_in"], sems, 6, "ctx", False)
    grad_route = lax.dot_general(
        grad_logits,
        two.astype(jnp.float32),
        ROWS_IN,
        precision=highest,
        preferred_element_type=jnp.float32,
    )
    r["g_small"][2:] = grad_route
    r["g_small"][1:2] = grad_gain_two
    finish(copies)
    mid_all = load_rows(r["mid_in"])
    grad_attended = low(dot_f32(mid_all, r["w_mix"][...], COLS_IN))
    grad_qkv = attend_back(r["qkv"], grad_attended, r["bias"], r["diag"], heads)
    store_tiles(r["norm_out"], low(dot_f32(grad_qkv, r["w_qkv"][...], COLS_IN)))
    copies = begin(r["norm_out"], r["norm_in"], sems, 7, "ctx", True)
    r["g_mix"][...] = dot_f32(r["attended"][...], mid_all, ROWS_IN)
    r["g_qkv"][...] = dot_f32(r["normed"][...], grad_qkv, ROWS_IN)
    finish(copies)
    grad_input, grad_gain_one = rms_norm_back(resid_in, gain_one, sum_tiles(r["norm_in"]))
    r["g_small"][0:1] = grad_gain_one
    r["grad_in"][...] = low(grad_input + grad_mid)


def layer_call(mode, heads, ctx_count, hd_count, operands):
    rows, width = operands["x"].shape
    experts = operands["small"].shape[0] - 2
    length, group = rows * ctx_count, heads * HD
    capacity = max(2, 2 * rows // experts)
    slots = experts * capacity
    total = slots * hd_count
    wide = 2 * width if mode == "both" else width
    b16, f32 = jnp.bfloat16, jnp.float32
    saved = {
        "normed": ((length, width), b16),
        "qkv": ((length, 3 * group), b16),
        "attended": ((length, group), b16),
        "mid": ((rows, width), f32),
        "two": ((rows, width), b16),
        "probs": ((rows, experts), f32),
        "gate": ((rows, 1), f32),
        "disp": ((rows, slots), b16),
        "routed": ((total, width), b16),
        "hidden": ((total, operands["w_in"].shape[1]), f32),
        "result": ((rows, width), f32),
    }
    grads = {
        "g_in": ((width, operands["w_in"].shape[1]), f32),
        "g_out": ((operands["w_out"].shape[0], width), f32),
        "g_qkv": ((width, 3 * group), f32),
        "g_mix": ((group, width), f32),
        "g_small": ((2 + experts, width), f32),
        "diag": ((heads + -heads % 8, 2 * length), f32),
        "grad_in": ((rows, width), b16),
    }
    scratch = {
        "slot_out": ((ctx_count, capacity, wide), b16),
        "slot_in": ((ctx_count, capacity, wide), b16),
        "mine": ((slots, wide), b16),
        "gathered": ((hd_count, slots, wide), b16),
        "term_out": ((hd_count, slots, wide), b16),
        "term_in": ((hd_count, slots, wide), b16),
        "back_out": ((ctx_count, capacity, wide), b16),
        "back_in": ((ctx_count, capacity, wide), b16),
    }
    outs = {}
    if mode != "back":
        outs["produced"] = ((rows, width), b16)
        scratch["all_x"] = ((ctx_count, rows, width), b16)
        scratch["mix_out"] = ((ctx_count, rows, width), b16)
        scratch["mix_in"] = ((ctx_count, rows, width), b16)
    if mode == "fwd":
        outs.update(saved)
    if mode == "both":
        scratch.update(saved)
    if mode != "fwd":
        outs.update(grads)
        units = operands["w_in"].shape[1]
        scratch["active"] = ((total, units), b16)
        scratch["grad_hidden"] = ((total, units), b16)
        scratch["grad_result"] = ((total, width), b16)
        scratch["mid_out"] = ((rows, width), b16)
        scratch["mid_in"] = ((ctx_count, rows, width), b16)
        scratch["norm_out"] = ((ctx_count, rows, width), b16)
        scratch["norm_in"] = ((ctx_count, rows, width), b16)
    names_in, names_out = tuple(operands), tuple(outs)
    names_scratch = tuple(scratch) + ("sems",)
    peers = max(ctx_count, hd_count) - 1
    results = pl.pallas_call(
        functools.partial(layer_kernel, mode, heads, names_in, names_out, names_scratch),
        out_shape=[jax.ShapeDtypeStruct(*outs[name]) for name in names_out],
        in_specs=[pl.BlockSpec(memory_space=pltpu.VMEM)] * len(names_in),
        out_specs=[pl.BlockSpec(memory_space=pltpu.VMEM)] * len(names_out),
        scratch_shapes=[pltpu.VMEM(*scratch[name]) for name in scratch]
        + [pltpu.SemaphoreType.DMA((8, 2, peers))],
        compiler_params=pltpu.CompilerParams(
            collective_id={"fwd": 0, "both": 1, "back": 2}[mode],
            has_side_effects=True,
            vmem_limit_bytes=56 * 2**20,
        ),
        name="layer_" + mode,
    )(*operands.values())
    return dict(zip(names_out, results))


def on_device_heads(
    tokens_in,
    grad_out,
    w_query,
    w_key,
    w_value,
    w_output,
    gain_attn,
    gain_ffn,
    router,
    rel_bias,
    w_in,
    w_out,
    routes,
    relative_bucket,
):
    section = lax.axis_index("section")
    is_first = section == 0
    ctx_count, hd_count = lax.axis_size("ctx"), lax.axis_size("hd")
    ctx_index = lax.axis_index("ctx")
    row_count, width = tokens_in.shape[1:]
    share = w_query.shape[1]
    heads = H // ctx_count
    group = heads * HD
    expert_count = router.shape[2]
    capacity = max(2, 2 * row_count // expert_count)
    slot_total = expert_count * capacity
    length = (relative_bucket.shape[0] + 1) // 2
    bias_share = rel_bias.shape[1]
    bucket_count = bias_share * ctx_count * hd_count // H

    qkv_tiles = jnp.concatenate(
        [w[0].reshape(share, ctx_count, 1, group) for w in (w_query, w_key, w_value)], axis=2
    ).transpose(1, 0, 2, 3)
    qkv_tiles = exchange(qkv_tiles.reshape(ctx_count, share, 3 * group), "ctx")
    qkv_own = gather_over(qkv_tiles, "hd").transpose(1, 0, 2, 3).reshape(width, 3 * group)
    mix_own = gather_over(w_output[0], "hd").reshape(group, width)
    w_qkv = gather_over(qkv_own, "section")
    w_mix = gather_over(mix_own, "section")
    experts_in = gather_over(w_in[0, 0], "section")
    experts_out = gather_over(w_out[0, 0], "section")
    bias_padded = jnp.pad(rel_bias[0], (0, share - bias_share))
    small = jnp.concatenate(
        [router[0], gain_attn[0][:, None], gain_ffn[0][:, None], bias_padded[:, None]], axis=1
    )
    small = gather_over(small, ("section", "ctx", "hd")).reshape(2, ctx_count * hd_count, share, -1)
    w_route = small[..., :expert_count].reshape(2, width, expert_count)
    gains = small[..., expert_count : expert_count + 2].astype(jnp.float32).reshape(2, width, 2)
    all_bias = small[:, :, :bias_share, expert_count + 2].reshape(2, H, bucket_count)
    own_bias = lax.dynamic_slice_in_dim(all_bias, ctx_index * heads, heads, 1)
    buckets = jnp.concatenate(
        [relative_bucket[:length][::-1], relative_bucket[:1], relative_bucket[length:][::-1]]
    )
    marks = (jnp.arange(bucket_count, dtype=jnp.int32)[:, None] == buckets[None]).astype(jnp.bfloat16)
    bias_rows = jnp.einsum("lhb,bm->lhm", own_bias, marks, preferred_element_type=jnp.float32)
    bias_rows = jnp.pad(bias_rows, ((0, 0), (0, -heads % 8), (0, 0)))
    diag_buckets = jnp.concatenate([relative_bucket[::-1], relative_bucket[:1] * 0 - 1])
    diag_marks = (
        jnp.arange(bucket_count, dtype=jnp.int32)[:, None] == diag_buckets[None]
    ).astype(jnp.float32)

    own_routes = exchange(routes[0][:, :, 0][:, None], "section")[:, 0]

    tokens = jnp.where(is_first, tokens_in[0], tokens_in[1])
    cotangent = jnp.where(is_first, grad_out[0], grad_out[1])

    layers = [
        {
            "small": jnp.concatenate(
                [gains[layer].T, w_route[layer].astype(jnp.float32).T], axis=0
            ),
            "bias": bias_rows[layer],
            "route": own_routes[layer][:, None],
            "w_qkv": w_qkv[layer],
            "w_mix": w_mix[layer],
            "w_in": experts_in[layer],
            "w_out": experts_out[layer],
        }
        for layer in range(2)
    ]
    call = functools.partial(layer_call, heads=heads, ctx_count=ctx_count, hd_count=hd_count)
    first = call("fwd", operands={"x": tokens, **layers[0]})
    first_out = first.pop("produced")
    second = call("both", operands={"x": first_out, "cot": cotangent, **layers[1]})
    second_out, second_grad = second["produced"], second["grad_in"]
    back = call("back", operands={"x": tokens, "cot": second_grad, **layers[0], **first})
    first_grad = back["grad_in"]

    def parts(grads):
        bias = lax.dot_general(grads["diag"][:heads], diag_marks, COLS_IN, precision=highest)
        bias = lax.dynamic_update_slice_in_dim(
            jnp.zeros((H, bucket_count), jnp.float32), bias, ctx_index * heads, 0
        ).reshape(-1, bias_share)
        bias = jnp.pad(bias, ((0, 0), (0, share - bias_share))).reshape(1, -1)
        small = jnp.concatenate([grads["g_small"], bias], axis=0).T
        return (grads["g_in"], grads["g_out"], grads["g_qkv"], grads["g_mix"], small)

    first_parts, second_parts = parts(back), parts(second)

    def to_section(first_part, second_part):
        low = lambda v: v.astype(jnp.bfloat16)
        up = lax.ppermute(low(second_part), "section", [(0, 1)])
        down = lax.ppermute(low(first_part), "section", [(1, 0)])
        kept = jnp.where(is_first, first_part, second_part)
        return kept + jnp.where(is_first, down, up).astype(jnp.float32)

    in_units, out_units, grad_stack, grad_mix, grad_small = (
        to_section(a, b) for a, b in zip(first_parts, second_parts)
    )
    stack_tiles = grad_stack.astype(jnp.bfloat16).reshape(ctx_count * hd_count, share, 3 * group)
    stack_tiles = exchange(stack_tiles, ("ctx", "hd")).reshape(ctx_count, hd_count, share, 3, group)
    stack_sum = jnp.sum(stack_tiles.astype(jnp.float32), axis=1)
    stack_sum = stack_sum.transpose(2, 1, 0, 3).reshape(3, share, width)
    mix_sum = sum_over(grad_mix.reshape(hd_count, share, width), "hd")
    small_sum = sum_over(grad_small.reshape(ctx_count * hd_count, share, -1), ("ctx", "hd"))
    both_out = exchange(jnp.stack([first_out, second_out]), "section")
    both_grad = exchange(jnp.stack([first_grad, second_grad]), "section")
    return (
        both_out[None],
        both_grad[None],
        stack_sum[0][None],
        stack_sum[1][None],
        stack_sum[2][None],
        mix_sum[None],
        small_sum[:, 0][None],
        small_sum[:, 1][None],
        small_sum[:, 2 : 2 + expert_count][None],
        small_sum[:bias_share, expert_count + 2][None],
        in_units[None, None],
        out_units[None, None],
    )


def solution(mesh):
    in_specs = (
        P(None, ("ctx", "hd"), None),
        P(None, ("ctx", "hd"), None),
        P("section", ("ctx", "hd"), None),
        P("section", ("ctx", "hd"), None),
        P("section", ("ctx", "hd"), None),
        P("section", ("ctx", "hd"), None),
        P("section", ("ctx", "hd")),
        P("section", ("ctx", "hd")),
        P("section", ("ctx", "hd"), None),
        P("section", ("ctx", "hd")),
        P("section", "ctx", None, "hd"),
        P("section", "ctx", "hd", None),
        P("section", None, ("ctx", "hd"), None),
        P(),
    )
    out_specs = (
        P("section", None, ("ctx", "hd"), None),
        P("section", None, ("ctx", "hd"), None),
        P("section", ("ctx", "hd"), None),
        P("section", ("ctx", "hd"), None),
        P("section", ("ctx", "hd"), None),
        P("section", ("ctx", "hd"), None),
        P("section", ("ctx", "hd")),
        P("section", ("ctx", "hd")),
        P("section", ("ctx", "hd"), None),
        P("section", ("ctx", "hd")),
        P("section", "ctx", None, "hd"),
        P("section", "ctx", "hd", None),
    )
    by_heads = H % mesh.shape["ctx"] == 0
    return jax.shard_map(
        on_device_heads if by_heads else on_device, mesh=mesh, in_specs=in_specs, out_specs=out_specs, check_vma=False
    )
```

```python
import functools
import math
import types

import jax
import jax.numpy as jnp
from jax import lax
from jax.experimental import pallas as pl
from jax.experimental.pallas import tpu as pltpu
from jax.sharding import PartitionSpec as P

H = 12
HD = 64
MB = 2
HEADS, CTX, SECTION = "hd", "ctx", "section"
FWD, BOTH, BACK = "fwd", "both", "back"
GATHERED, ALL_X = "gathered", "all_x"


epsilon = 1e-06
highest = lax.Precision.HIGHEST


def from_behind(value, axis, steps):
    count = lax.axis_size(axis)
    first, last = (max(0, -steps), min(count, count - steps))
    return lax.ppermute(value, axis, [(source, source + steps) for source in range(first, last)])


def split_up(value, dim, size):
    shape = value.shape
    tiles = value.reshape(*shape[:dim], size, shape[dim] // size, *shape[dim + 1 :])
    return jnp.moveaxis(tiles, dim, 0)


def summed_on_arrival(value, axis, dim):
    size = lax.axis_size(axis)
    tiles = lax.all_to_all(split_up(value, dim, size), axis, 0, 0, tiled=True)
    return jnp.sum(tiles.astype(jnp.float32), axis=0)


def in_one_piece(arrays, axis, dim, along):
    columns = [a.reshape(*a.shape[:along], -1) for a in arrays]
    both = jnp.concatenate(columns, axis=along)
    out, at, outs = (summed_on_arrival(both, axis, dim), 0, [])
    for a, column in zip(arrays, columns):
        section = out[..., at : at + column.shape[along]]
        outs.append(section.reshape(*section.shape[:along], *a.shape[along:]))
        at += column.shape[along]
    return tuple(outs)


def rms_norm(hidden, gain):
    return hidden * lax.rsqrt(jnp.mean(hidden * hidden, axis=-1, keepdims=True) + epsilon) * gain


def over_blocks(update, running, stacked_arrays):
    row_span = stacked_arrays.shape[2]
    block_rows = math.gcd(row_span, 512)

    def advance(inner_state, block_index):
        first_row = block_index * block_rows
        portion = lax.dynamic_slice_in_dim(stacked_arrays, first_row, block_rows, 2)
        return (update(inner_state, portion, first_row), None)

    running, _ = lax.scan(advance, running, jnp.arange(row_span // block_rows, dtype=jnp.int32))
    return running


def bucket_lookup(relative_bucket, query_pos, key_pos):
    length = (relative_bucket.shape[0] + 1) // 2
    return jnp.take(relative_bucket, query_pos[:, None] - key_pos[None, :] + (length - 1))


def scores_of(queries, key_block, bias_table, bucket_ids):
    raw = jnp.einsum("sqhd,skhd->shqk", queries, key_block, preferred_element_type=jnp.float32)
    return raw * queries.shape[-1] ** (-0.5) + jnp.take(bias_table, bucket_ids, axis=1)[None]


def score_grads(
    queries, grad_heads, logsumexp_total, row_delta, key_block, value_block, bias_table, bucket_ids
):
    scores = scores_of(queries, key_block, bias_table, bucket_ids)
    weights = jnp.exp(scores - logsumexp_total[..., None])
    grad_weights = jnp.einsum(
        "sqhd,skhd->shqk", grad_heads, value_block, preferred_element_type=jnp.float32
    )
    score_gradient = (weights * (grad_weights - row_delta[..., None])).astype(jnp.bfloat16)
    return (score_gradient, weights.astype(jnp.bfloat16))


def bias_grad(score_gradient, bucket_ids, bucket_count):
    marker_flags = (
        bucket_ids[None] == jnp.arange(bucket_count, dtype=jnp.int32)[:, None, None]
    ).astype(jnp.bfloat16)
    return jnp.einsum(
        "shqk,mqk->hm", score_gradient, marker_flags, preferred_element_type=jnp.float32
    )


def to_heads(stacked_arrays):
    return lax.all_to_all(stacked_arrays, HEADS, split_axis=3, concat_axis=1, tiled=True)


def to_rows(stacked_arrays):
    return lax.all_to_all(stacked_arrays, HEADS, split_axis=1, concat_axis=3, tiled=True)


def cycle_fold(stacked_arrays, update, running):
    return over_blocks(update, running, lax.all_gather(stacked_arrays, CTX, axis=2, tiled=True))


def expert_swap(slots):
    return lax.all_to_all(slots, CTX, split_axis=0, concat_axis=0, tiled=True)


def expert_gather(slots):
    return lax.all_gather(slots, HEADS, axis=0, tiled=True)


def expert_sum(term, row_total):
    return lax.psum_scatter(
        term(jnp.int32(0), row_total * lax.axis_size(HEADS)).astype(jnp.bfloat16),
        HEADS,
        scatter_dimension=0,
        tiled=True,
    ).astype(jnp.float32)


def on_device(
    tokens_in,
    grad_out,
    w_query,
    w_key,
    w_value,
    w_output,
    gain_attn,
    gain_ffn,
    router,
    rel_bias,
    w_in,
    w_out,
    routes,
    relative_bucket,
):
    is_first = lax.axis_index(SECTION) == 0
    hd_count = lax.axis_size(HEADS)
    head_group = H // hd_count
    gathered_weights = (
        lax.all_gather(w_query, (CTX, HEADS), axis=1, tiled=True),
        lax.all_gather(w_key, (CTX, HEADS), axis=1, tiled=True),
        lax.all_gather(w_value, (CTX, HEADS), axis=1, tiled=True),
        lax.all_gather(w_output, (CTX, HEADS), axis=1, tiled=True),
        lax.all_gather(gain_attn, (CTX, HEADS), axis=1, tiled=True),
        lax.all_gather(gain_ffn, (CTX, HEADS), axis=1, tiled=True),
        lax.all_gather(router, (CTX, HEADS), axis=1, tiled=True),
        lax.all_gather(rel_bias, (CTX, HEADS), axis=1, tiled=True),
    )
    w_stack = jnp.stack([gathered_weights[0][0], gathered_weights[1][0], gathered_weights[2][0]])
    w_mix = gathered_weights[3][0]
    gain_first = gathered_weights[4][0].astype(jnp.float32)
    gain_second = gathered_weights[5][0].astype(jnp.float32)
    w_route = gathered_weights[6][0]
    bucket_count = gathered_weights[7].shape[1] // H
    all_bias = gathered_weights[7][0].astype(jnp.float32).reshape(H, bucket_count)
    bias_table = lax.dynamic_slice_in_dim(
        all_bias, lax.axis_index(HEADS) * head_group, head_group, 0
    )
    expert_in = w_in[0, 0]
    expert_out = w_out[0, 0]
    row_count = tokens_in.shape[1]
    query_pos = lax.axis_index(CTX) * row_count + jnp.arange(row_count, dtype=jnp.int32)
    expert_count = router.shape[2]
    capacity = max(2, 2 * row_count // expert_count)
    slot_total = expert_count * capacity
    length = (relative_bucket.shape[0] + 1) // 2
    scale = HD ** (-0.5)
    group_width = head_group * HD
    contract_rows = (((0,), (0,)), ((), ()))
    contract_cols = (((1,), (1,)), ((), ()))

    def backward(saved, cotangent):
        (
            resid_in,
            normed,
            grouped,
            logsumexp_total,
            attended_full,
            attended,
            resid_mid,
            normed_two,
            router_probs,
            gate_value,
            chosen,
            dispatch,
            routed_rows,
            hidden,
            active,
            combined,
        ) = saved
        grad_gate = jnp.sum(cotangent * combined, axis=-1)
        grad_logits = router_probs * (
            jnp.where(chosen, grad_gate[:, None], 0.0) - (gate_value * grad_gate)[:, None]
        )
        grad_router = lax.dot_general(
            normed_two.astype(jnp.float32), grad_logits, contract_rows, precision=highest
        )
        grad_normed = lax.dot_general(
            grad_logits, w_route.astype(jnp.float32), contract_cols, precision=highest
        )
        grad_slots = jnp.dot(
            dispatch.astype(jnp.float32), gate_value[:, None] * cotangent, precision=highest
        ).astype(jnp.bfloat16)
        grad_arrived = expert_swap(grad_slots.reshape(expert_count, capacity, -1))
        grad_result = expert_gather(grad_arrived).reshape(-1, cotangent.shape[1])
        grad_active = lax.dot_general(
            grad_result, expert_out, contract_cols, preferred_element_type=jnp.float32
        )
        gelu_back = jax.vjp(jax.nn.gelu, hidden)[1]
        grad_hidden = gelu_back(grad_active)[0].astype(jnp.bfloat16)
        grad_expert_out = lax.dot_general(
            active, grad_result, contract_rows, preferred_element_type=jnp.float32
        )
        grad_expert_in = lax.dot_general(
            routed_rows, grad_hidden, contract_rows, preferred_element_type=jnp.float32
        )

        def in_term(offset, row_span):
            return lax.dot_general(
                grad_hidden, expert_in, contract_cols, preferred_element_type=jnp.float32
            )

        grad_routed = expert_sum(in_term, grad_arrived.shape[0] * capacity).astype(jnp.bfloat16)
        grad_returned = expert_swap(
            grad_routed.reshape(-1, capacity, grad_routed.shape[1])
        ).reshape(slot_total, -1)
        grad_normed = grad_normed + lax.dot_general(
            dispatch, grad_returned, contract_rows, preferred_element_type=jnp.float32
        )
        norm_back = jax.vjp(rms_norm, resid_mid, gain_second)[1]
        grad_mid, grad_gain_second = norm_back(grad_normed)
        grad_mid = grad_mid + cotangent
        grad_mix = lax.dot_general(
            attended.astype(jnp.float32), grad_mid, contract_rows, precision=highest
        )
        grad_attended = lax.dot_general(
            grad_mid, w_mix.astype(jnp.float32), contract_cols, precision=highest
        ).astype(jnp.bfloat16)
        grad_heads = to_heads(grad_attended[None, None])[0]
        queries = grouped[0].reshape(hd_count, row_count, head_group, HD)
        grad_query_heads = grad_heads.reshape(hd_count, row_count, head_group, HD)
        row_delta = jnp.einsum(
            "sqhd,sqhd->shq", grad_query_heads.astype(jnp.float32), attended_full
        )

        def summed_update(running, portion, offset):
            query_sum, bias_sum, key_sums = running
            key_block = portion[0].reshape(hd_count, -1, head_group, HD)
            value_block = portion[1].reshape(hd_count, -1, head_group, HD)
            span = portion.shape[2]
            bucket_ids = bucket_lookup(
                relative_bucket, query_pos, offset + jnp.arange(span, dtype=jnp.int32)
            )
            score_gradient, weights = score_grads(
                queries,
                grad_query_heads,
                logsumexp_total,
                row_delta,
                key_block,
                value_block,
                bias_table,
                bucket_ids,
            )
            query_sum = query_sum + jnp.einsum(
                "shqk,skhd->sqhd", score_gradient, key_block, preferred_element_type=jnp.float32
            )
            bias_sum = bias_sum + bias_grad(score_gradient, bucket_ids, bucket_count)
            key_part = jnp.einsum(
                "shqk,sqhd->skhd", score_gradient, queries, preferred_element_type=jnp.float32
            )
            value_part = jnp.einsum(
                "shqk,sqhd->skhd", weights, grad_query_heads, preferred_element_type=jnp.float32
            )
            fresh = jnp.stack([key_part, value_part]).reshape(2, hd_count, span, group_width)
            current = lax.dynamic_slice_in_dim(key_sums, offset, span, 2)
            key_sums = lax.dynamic_update_slice_in_dim(key_sums, current + fresh, offset, 2)
            return (query_sum, bias_sum, key_sums)

        start_grads = (
            jnp.zeros((hd_count, row_count, head_group, HD), jnp.float32),
            jnp.zeros((head_group, bucket_count), jnp.float32),
            jnp.zeros((2, hd_count, length, group_width), jnp.float32),
        )
        query_sum, bias_sum, key_sums = cycle_fold(grouped[1:3], summed_update, start_grads)
        key_grads = lax.psum_scatter(
            key_sums.astype(jnp.bfloat16), CTX, scatter_dimension=2, tiled=True
        ).astype(jnp.float32)
        grad_qkv = jnp.stack(
            [
                (query_sum * scale).reshape(hd_count, row_count, group_width),
                key_grads[0] * scale,
                key_grads[1],
            ]
        ).astype(jnp.bfloat16)
        grad_rows = to_rows(grad_qkv)[:, 0]
        grad_stack = jnp.einsum(
            "rd,sre->sde", normed, grad_rows, preferred_element_type=jnp.float32
        )
        grad_normed_one = jnp.einsum(
            "sre,sde->rd", grad_rows, w_stack, preferred_element_type=jnp.float32
        )
        norm_back_one = jax.vjp(rms_norm, resid_in, gain_first)[1]
        grad_input, grad_gain_first = norm_back_one(grad_normed_one)
        grad_input = (grad_input + grad_mid).astype(jnp.bfloat16)
        return (
            grad_input,
            (
                grad_stack,
                grad_mix,
                grad_gain_first,
                grad_gain_second,
                grad_router,
                bias_sum,
                grad_expert_in,
                grad_expert_out,
            ),
        )

    received = jnp.zeros((row_count, tokens_in.shape[2]), jnp.bfloat16)
    saved_list = []
    produced_list = []
    for tick_index in range(MB + 1):
        section_input = jnp.where(is_first, tokens_in[min(tick_index, MB - 1)], received)
        route_ids = jnp.where(
            is_first,
            routes[0, min(tick_index, MB - 1), :, 0],
            routes[0, max(tick_index - 1, 0), :, 0],
        )
        forward_resid_in = section_input.astype(jnp.float32)
        forward_normed = rms_norm(forward_resid_in, gain_first).astype(jnp.bfloat16)
        projected = jnp.einsum(
            "rd,sde->sre", forward_normed, w_stack, preferred_element_type=jnp.float32
        ).astype(jnp.bfloat16)
        forward_grouped = to_heads(projected[:, None])
        forward_queries = forward_grouped[0].reshape(hd_count, row_count, head_group, HD)

        def stats_update(running, portion, offset):
            row_max, row_sum = running
            key_pos = offset + jnp.arange(portion.shape[2], dtype=jnp.int32)
            scores = scores_of(
                forward_queries,
                portion[0].reshape(hd_count, -1, head_group, HD),
                bias_table,
                bucket_lookup(relative_bucket, query_pos, key_pos),
            )
            new_max = jnp.maximum(row_max, jnp.max(scores, axis=-1))
            row_sum = row_sum * jnp.exp(row_max - new_max) + jnp.sum(
                jnp.exp(scores - new_max[..., None]), axis=-1
            )
            return (new_max, row_sum)

        start_stats = (
            jnp.full((hd_count, head_group, row_count), -1e30, jnp.float32),
            jnp.zeros((hd_count, head_group, row_count), jnp.float32),
        )
        row_max, row_sum = cycle_fold(forward_grouped[1:2], stats_update, start_stats)
        forward_logsumexp_total = row_max + jnp.log(row_sum)

        def value_update(running, portion, offset):
            key_pos = offset + jnp.arange(portion.shape[2], dtype=jnp.int32)
            scores = scores_of(
                forward_queries,
                portion[0].reshape(hd_count, -1, head_group, HD),
                bias_table,
                bucket_lookup(relative_bucket, query_pos, key_pos),
            )
            weights = jnp.exp(scores - forward_logsumexp_total[..., None]).astype(jnp.bfloat16)
            return running + jnp.einsum(
                "shqk,skhd->sqhd",
                weights,
                portion[1].reshape(hd_count, -1, head_group, HD),
                preferred_element_type=jnp.float32,
            )

        forward_attended_full = cycle_fold(
            forward_grouped[1:3],
            value_update,
            jnp.zeros((hd_count, row_count, head_group, HD), jnp.float32),
        )
        forward_attended = to_rows(
            forward_attended_full.reshape(1, hd_count, row_count, group_width).astype(jnp.bfloat16)
        )[0, 0]
        forward_resid_mid = forward_resid_in + jnp.dot(
            forward_attended, w_mix, preferred_element_type=jnp.float32
        )
        forward_normed_two = rms_norm(forward_resid_mid, gain_second).astype(jnp.bfloat16)
        forward_router_probs = jax.nn.softmax(
            jnp.dot(forward_normed_two, w_route, preferred_element_type=jnp.float32), axis=-1
        )
        forward_chosen = route_ids[:, None] == jnp.arange(expert_count, dtype=jnp.int32)[None, :]
        forward_gate_value = jnp.sum(jnp.where(forward_chosen, forward_router_probs, 0.0), axis=-1)
        chosen_int = forward_chosen.astype(jnp.int32)
        slot_rank = jnp.sum((jnp.cumsum(chosen_int, axis=0) - chosen_int) * chosen_int, axis=-1)
        slot_index = route_ids * capacity + slot_rank
        forward_dispatch = (
            jnp.arange(slot_total, dtype=jnp.int32)[:, None] == slot_index[None, :]
        ).astype(jnp.bfloat16)
        outgoing = jnp.dot(
            forward_dispatch, forward_normed_two, preferred_element_type=jnp.float32
        ).astype(jnp.bfloat16)
        arrived = expert_swap(outgoing.reshape(expert_count, capacity, -1))
        forward_routed_rows = expert_gather(arrived).reshape(-1, forward_normed_two.shape[1])
        forward_hidden = jnp.dot(forward_routed_rows, expert_in, preferred_element_type=jnp.float32)
        forward_active = jax.nn.gelu(forward_hidden).astype(jnp.bfloat16)

        def out_term(offset, row_span):
            return jnp.dot(forward_active, expert_out, preferred_element_type=jnp.float32)

        result = expert_sum(out_term, arrived.shape[0] * capacity).astype(jnp.bfloat16)
        returned = expert_swap(result.reshape(-1, capacity, result.shape[1])).reshape(
            slot_total, -1
        )
        forward_combined = lax.dot_general(
            forward_dispatch, returned, contract_rows, preferred_element_type=jnp.float32
        )
        section_output = (
            forward_resid_mid + forward_gate_value[:, None] * forward_combined
        ).astype(jnp.bfloat16)
        forward_saved = (
            forward_resid_in,
            forward_normed,
            forward_grouped,
            forward_logsumexp_total,
            forward_attended_full,
            forward_attended,
            forward_resid_mid,
            forward_normed_two,
            forward_router_probs,
            forward_gate_value,
            forward_chosen,
            forward_dispatch,
            forward_routed_rows,
            forward_hidden,
            forward_active,
            forward_combined,
        )
        saved = forward_saved
        saved_list.append(saved)
        produced_list.append(section_output)
        if tick_index < MB:
            received = from_behind(section_output, SECTION, 1)
    incoming = jnp.zeros((row_count, tokens_in.shape[2]), jnp.float32)
    grad_total = None
    grad_list = []
    for tick_index in range(MB + 1):
        last_cot = (
            grad_out[max(MB - 1 - tick_index, 0)].astype(jnp.float32)
            if tick_index < MB
            else jnp.zeros_like(incoming)
        )
        cotangent = jnp.where(is_first, incoming, last_cot)
        grad_input, grad_parts = backward(saved_list[MB - tick_index], cotangent)
        grad_total = (
            grad_parts if grad_total is None else jax.tree.map(jnp.add, grad_total, grad_parts)
        )
        grad_list.append(grad_input)
        if tick_index < MB:
            incoming = from_behind(grad_input, SECTION, -1).astype(jnp.float32)
    section_rows = jnp.stack(
        [
            jnp.where(is_first, produced_list[micro_index], produced_list[micro_index + 1])
            for micro_index in range(MB)
        ]
    )[None]
    grad_rows_out = jnp.stack(
        [
            jnp.where(is_first, grad_list[MB - micro_index], grad_list[MB - 1 - micro_index])
            for micro_index in range(MB)
        ]
    )[None]
    (
        grad_stack,
        grad_mix,
        grad_gain_first,
        grad_gain_second,
        grad_router,
        bias_sum,
        grad_expert_in,
        grad_expert_out,
    ) = grad_total
    bias_full = lax.dynamic_update_slice_in_dim(
        jnp.zeros((H, bucket_count), jnp.float32), bias_sum, lax.axis_index(HEADS) * head_group, 0
    )
    summed_grads = (
        *in_one_piece(
            (
                grad_stack[0].astype(jnp.bfloat16),
                grad_stack[1].astype(jnp.bfloat16),
                grad_stack[2].astype(jnp.bfloat16),
                grad_mix.astype(jnp.bfloat16),
                grad_gain_first.astype(jnp.bfloat16),
                grad_gain_second.astype(jnp.bfloat16),
                grad_router.astype(jnp.bfloat16),
            ),
            (CTX, HEADS),
            0,
            1,
        ),
        summed_on_arrival(bias_full.reshape(-1).astype(jnp.bfloat16), (CTX, HEADS), 0),
    )
    return (
        section_rows,
        grad_rows_out,
        summed_grads[0][None],
        summed_grads[1][None],
        summed_grads[2][None],
        summed_grads[3][None],
        summed_grads[4][None],
        summed_grads[5][None],
        summed_grads[6][None],
        summed_grads[7][None],
        grad_expert_in[None, None],
        grad_expert_out[None, None],
    )


def dot_f32(a, b, dims=(((1,), (0,)), ((), ()))):
    return lax.dot_general(a, b, dims, preferred_element_type=jnp.float32)


ROWS_IN = (((0,), (0,)), ((), ()))
COLS_IN = (((1,), (1,)), ((), ()))


def toeplitz(vec_row, length):
    wide = jnp.broadcast_to(vec_row, (length, 2 * length))
    return pltpu.roll(wide, 0, 1, stride=1, stride_axis=0)[:, :length]


MESH_ID = pl.DeviceIdType.MESH


def greet(axes):
    barrier = pltpu.get_barrier_semaphore()
    total = 0
    for axis in axes:
        me, count = lax.axis_index(axis), lax.axis_size(axis)
        for step in range(1, count):
            peer = lax.rem(me + step, count)
            pl.semaphore_signal(barrier, inc=1, device_id={axis: peer}, device_id_type=MESH_ID)
            total += 1
    pl.semaphore_wait(barrier, total)


class Sender:
    def __init__(self, sems):
        self.sems, self.used = sems, 0

    def push(self, axis, source, target, keep=None):
        me, count = lax.axis_index(axis), lax.axis_size(axis)
        copies = []
        for step in range(1, count):
            peer = lax.rem(me + step, count)
            copy = self.send(axis, peer, source(peer), target(me))
            copies.append(copy)
        if keep is None:
            target(me)[...] = source(me)[...]
        return copies

    def send(self, axis, peer, source, target):
        copy = pltpu.make_async_remote_copy(
            src_ref=source,
            dst_ref=target,
            send_sem=self.sems.at[self.used, 0],
            recv_sem=self.sems.at[self.used, 1],
            device_id={axis: peer},
            device_id_type=MESH_ID,
        )
        self.used += 1
        copy.start()
        return copy

    def spread(self, axis, src, dst):
        return self.push(axis, lambda peer: src.at[peer], lambda me: dst.at[me])

    def share(self, axis, src, dst):
        return self.push(axis, lambda peer: src, lambda me: dst.at[me])


def finish(copies):
    for copy in copies:
        copy.wait()


def store_tiles(ref, value):
    for tile in range(ref.shape[0]):
        ref[tile] = value[tile * ref.shape[1] : (tile + 1) * ref.shape[1]]


def load_rows(ref):
    return ref[...].reshape(ref.shape[0] * ref.shape[1], ref.shape[2])


def sum_tiles(ref):
    total = ref[0].astype(jnp.float32)
    for tile in range(1, ref.shape[0]):
        total = total + ref[tile].astype(jnp.float32)
    return total


def rms_norm_back(hidden, gain, grad):
    inverse = lax.rsqrt(jnp.mean(hidden * hidden, axis=-1, keepdims=True) + epsilon)
    scaled = gain * grad
    mean = jnp.mean(hidden * scaled, axis=-1, keepdims=True)
    gain_grad = jnp.sum(hidden * inverse * grad, axis=0, keepdims=True)
    return inverse * scaled - hidden * (inverse * inverse * inverse * mean), gain_grad


def gelu_parts(u):
    scale = math.sqrt(2.0 / math.pi)
    t = jnp.tanh(scale * (u + 0.044715 * (u * u * u)))
    slope = 0.5 * (1.0 + t) + 0.5 * u * (1.0 - t * t) * scale * (1.0 + 3 * 0.044715 * u * u)
    return 0.5 * u * (1.0 + t), slope


def softmax_parts(qkv, bias_ref, head, heads):
    length = qkv.shape[0]
    width = heads * HD
    at = head * HD
    q = qkv[:, at : at + HD]
    k = qkv[:, width + at : width + at + HD]
    v = qkv[:, 2 * width + at : 2 * width + at + HD]
    scores = dot_f32(q, k, COLS_IN) * HD ** (-0.5) + toeplitz(bias_ref[head : head + 1], length)
    powers = jnp.exp(scores - jnp.max(scores, axis=-1, keepdims=True))
    return q, k, v, powers / jnp.sum(powers, axis=-1, keepdims=True)


def attend(qkv, bias_ref, heads):
    outs = []
    for head in range(heads):
        _, _, v, weights = softmax_parts(qkv, bias_ref, head, heads)
        outs.append(dot_f32(weights.astype(jnp.bfloat16), v))
    return jnp.concatenate(outs, axis=1).astype(jnp.bfloat16)


def attend_back(qkv, grads, bias_ref, diag_ref, heads):
    length = qkv.shape[0]
    rows = lax.broadcasted_iota(jnp.int32, (length, length), 0)
    cols = lax.broadcasted_iota(jnp.int32, (length, length), 1)
    flip = jnp.where(rows + cols == length - 1, 1.0, 0.0).astype(jnp.bfloat16)
    dqs, dks, dvs = [], [], []
    diag_ref[...] = jnp.zeros_like(diag_ref)
    for head in range(heads):
        q, k, v, weights = softmax_parts(qkv, bias_ref, head, heads)
        grad = grads[:, head * HD : (head + 1) * HD]
        grad_weights = dot_f32(grad, v, COLS_IN)
        delta = jnp.sum(weights * grad_weights, axis=-1, keepdims=True)
        score_grad = (weights * (grad_weights - delta)).astype(jnp.bfloat16)
        dqs.append(dot_f32(score_grad, k) * HD ** (-0.5))
        dks.append(dot_f32(score_grad, q, ROWS_IN) * HD ** (-0.5))
        dvs.append(dot_f32(weights.astype(jnp.bfloat16), grad, ROWS_IN))
        flipped = dot_f32(flip, score_grad)
        wide = jnp.concatenate([flipped, jnp.zeros_like(flipped)], axis=1)
        rolled = pltpu.roll(wide, 0, 1, stride=1, stride_axis=0)
        diag_ref[head : head + 1] = jnp.sum(rolled, axis=0, keepdims=True)
    return jnp.concatenate(dqs + dks + dvs, axis=1).astype(jnp.bfloat16)


SAVED = ("normed", "qkv", "attended", "mid", "two", "probs", "gate", "disp", "hidden", "result")


def load_weight(ref):
    return ref[...].reshape(-1, ref.shape[-1])


def layer_pass(mode, heads, sender, r):
    rows, width = r.x.shape
    experts = r.experts
    gain_one = r.small[0:1]
    gain_two = r.small[1:2]
    low = lambda v: v.astype(jnp.bfloat16)

    if mode != BACK:
        copies = r.x_copies or sender.share(CTX, r.x, r.all_x)
        resid_in = r.x[...].astype(jnp.float32)
        finish(copies)
        normed = low(rms_norm(load_rows(r.all_x).astype(jnp.float32), gain_one))
        r.normed[...] = normed
        r.qkv[...] = low(dot_f32(normed, load_weight(r.w_qkv)))
        r.attended[...] = attend(r.qkv, r.bias, heads)
        store_tiles(r.mix_out, low(dot_f32(r.attended[...], load_weight(r.w_mix))))
        copies = sender.spread(CTX, r.mix_out, r.mix_in)
        route = r.route[...]
        chosen = jnp.where(
            lax.broadcasted_iota(jnp.int32, (rows, experts), 1) == route, 1.0, 0.0
        )
        earlier = jnp.where(
            lax.broadcasted_iota(jnp.int32, (rows, rows), 0)
            > lax.broadcasted_iota(jnp.int32, (rows, rows), 1),
            1.0,
            0.0,
        )
        ranks = dot_f32(low(earlier), low(chosen))
        rank = jnp.sum(ranks * chosen, axis=-1, keepdims=True).astype(jnp.int32)
        slots = r.slot_out.shape[0] * r.slot_out.shape[1]
        slot_at = route * (slots // experts) + rank
        disp = low(
            jnp.where(lax.broadcasted_iota(jnp.int32, (rows, slots), 1) == slot_at, 1.0, 0.0)
        )
        r.disp[...] = disp
        finish(copies)
        mid = resid_in + sum_tiles(r.mix_in)
        two = low(rms_norm(mid, gain_two))
        logits = dot_f32(two, low(r.small[2 : 2 + experts]), COLS_IN)
        powers = jnp.exp(logits - jnp.max(logits, axis=-1, keepdims=True))
        probs = powers / jnp.sum(powers, axis=-1, keepdims=True)
        gate = jnp.sum(probs * chosen, axis=-1, keepdims=True)
        r.mid[...] = mid
        r.two[...] = two
        r.probs[...] = probs
        r.gate[...] = gate
    else:
        resid_in = r.x[...].astype(jnp.float32)
        mid, two, probs, gate = r.mid[...], r.two[...], r.probs[...], r.gate[...]
        disp = r.disp[...]
        route = r.route[...]
        chosen = jnp.where(
            lax.broadcasted_iota(jnp.int32, (rows, experts), 1) == route, 1.0, 0.0
        )

    r.before_experts()
    if mode != FWD:
        cotangent = r.cot[...].astype(jnp.float32)
        grad_rows = low(gate * cotangent)
    if mode == FWD:
        payload = two
    elif mode == BACK:
        payload = grad_rows
    else:
        payload = jnp.concatenate([two, grad_rows], axis=1)
    store_tiles(r.slot_out, low(dot_f32(disp, payload, ROWS_IN)))
    me, count = lax.axis_index(CTX), lax.axis_size(CTX)
    there = sender.spread(CTX, r.slot_out, r.slot_in)

    def chunk_at(step):
        return lax.rem(me + count - step, count)

    def send_on(step):
        chunk = chunk_at(step)
        return sender.push(
            HEADS, lambda p: r.slot_in.at[chunk], lambda at: r.gathered.at[chunk, at]
        )

    def send_back(step):
        chunk = chunk_at(step)
        finish(sums[step])
        total = r.term_in[pl.ds(chunk, 1), 0].astype(jnp.float32)
        for tile in range(1, r.term_in.shape[1]):
            total = total + r.term_in[pl.ds(chunk, 1), tile].astype(jnp.float32)
        if step == 0:
            r.back_in[pl.ds(me, 1)] = low(total)
            return []
        r.back_out[pl.ds(chunk, 1)] = low(total)
        return [sender.send(CTX, chunk, r.back_out.at[chunk], r.back_in.at[me])]

    gathers, sums, returns = [send_on(0)], [], []
    for step in range(count):
        chunk = chunk_at(step)
        if step + 1 < count:
            finish(there[step : step + 1])
            gathers.append(send_on(step + 1))
        finish(gathers[step])
        rows_here = r.gathered[pl.ds(chunk, 1)].reshape(-1, r.gathered.shape[-1])
        tile_shape = (1, *r.term_out.shape[1:3], width)
        if mode != BACK:
            hidden = dot_f32(rows_here[:, :width], r.w_in[...])
            r.hidden[pl.ds(chunk, 1)] = hidden[None]
        else:
            hidden = r.hidden[pl.ds(chunk, 1)][0]
        active, slope = gelu_parts(hidden)
        active = low(active)
        if mode != BACK:
            r.term_out[pl.ds(chunk, 1), :, :, :width] = low(
                dot_f32(active, r.w_out[...])
            ).reshape(tile_shape)
        if mode != FWD:
            r.active[pl.ds(chunk, 1)] = active[None]
            grad_hidden = low(slope * dot_f32(rows_here[:, -width:], r.w_out[...], COLS_IN))
            r.grad_hidden[pl.ds(chunk, 1)] = grad_hidden[None]
            r.term_out[pl.ds(chunk, 1), :, :, -width:] = low(
                dot_f32(grad_hidden, r.w_in[...], COLS_IN)
            ).reshape(tile_shape)
        sums.append(
            sender.push(
                HEADS,
                lambda p, chunk=chunk: r.term_out.at[chunk, p],
                lambda at, chunk=chunk: r.term_in.at[chunk, at],
            )
        )
        if step > 0:
            returns += send_back(step - 1)
    if mode != FWD:
        arrived = r.gathered[...].reshape(-1, r.gathered.shape[-1])
        r.put(False, dot_f32(load_rows(r.active), arrived[:, -width:], ROWS_IN))
    returns += send_back(count - 1)
    if mode != FWD:
        routed = r.routed[...].reshape(-1, r.routed.shape[-1])[:, :width]
        r.put(True, dot_f32(routed, load_rows(r.grad_hidden), ROWS_IN))
        r.after_units()
    finish(returns)
    returned = dot_f32(disp, load_rows(r.back_in))
    if mode != BACK:
        result = returned[:, :width]
        r.result[...] = result
        r.produced[...] = low(mid + gate * result)
    else:
        result = r.result[...]
    if mode == FWD:
        return

    grad_gate = jnp.sum(cotangent * result, axis=-1, keepdims=True)
    grad_logits = probs * (chosen - gate) * grad_gate
    grad_two = returned[:, -width:]
    for expert in range(experts):
        grad_two = grad_two + grad_logits[:, expert : expert + 1] * r.small[2 + expert : 3 + expert]
    grad_mid, grad_gain_two = rms_norm_back(mid, gain_two, grad_two)
    grad_mid = grad_mid + cotangent
    r.mid_out[...] = low(grad_mid)
    copies = sender.share(CTX, r.mid_out, r.mid_in)
    grad_route = lax.dot_general(
        grad_logits,
        two.astype(jnp.float32),
        ROWS_IN,
        precision=highest,
        preferred_element_type=jnp.float32,
    )
    r.g_small[2 : 2 + experts] = grad_route
    r.g_small[1:2] = grad_gain_two
    finish(copies)
    mid_all = load_rows(r.mid_in)
    grad_attended = low(dot_f32(mid_all, load_weight(r.w_mix), COLS_IN))
    grad_qkv = attend_back(r.qkv, grad_attended, r.bias, r.diag, heads)
    store_tiles(r.norm_out, low(dot_f32(grad_qkv, load_weight(r.w_qkv), COLS_IN)))
    copies = sender.spread(CTX, r.norm_out, r.norm_in)
    r.g_mix[...] = dot_f32(r.attended[...], mid_all, ROWS_IN)
    r.g_qkv[...] = dot_f32(r.normed[...], grad_qkv, ROWS_IN)
    finish(copies)
    grad_input, grad_gain_one = rms_norm_back(resid_in, gain_one, sum_tiles(r.norm_in))
    r.g_small[0:1] = grad_gain_one
    r.grad_in[...] = low(grad_input + grad_mid)


def step_kernel(heads, experts, names, *refs):
    *refs, sems = refs
    r = types.SimpleNamespace(**{n: ref for (g, n), ref in zip(names, refs) if g == 0})
    groups = {
        mode: {n: ref for (g, n), ref in zip(names, refs) if g == mode}
        for mode in (FWD, BOTH, BACK)
    }
    low = lambda v: v.astype(jnp.bfloat16)
    s = lax.axis_index(SECTION)
    other = 1 - s
    c = lax.axis_index(CTX)
    ctx_count, hd_count = lax.axis_size(CTX), lax.axis_size(HEADS)
    share = r.w_query.shape[0]
    group = heads * HD
    width = r.w_query.shape[1]
    sender = Sender(sems)
    greet((SECTION, CTX, HEADS))

    unit_copies = sender.push(
        SECTION, lambda p: r.w_in, lambda me: r.units_in.at[me], keep=False
    )
    unit_copies += sender.push(
        SECTION, lambda p: r.w_out, lambda me: r.units_out.at[me], keep=False
    )
    for tile in range(ctx_count):
        at = slice(tile * group, (tile + 1) * group)
        r.tile_out[tile] = jnp.concatenate(
            [ref[:, at] for ref in (r.w_query, r.w_key, r.w_value)], axis=1
        )
    copies = sender.spread(CTX, r.tile_out, r.tile_in)
    copies += sender.push(SECTION, lambda p: r.routes.at[p], lambda me: r.route.at[me])
    copies += sender.push(HEADS, lambda p: r.w_output, lambda me: r.w_mix.at[s, me])
    copies += sender.share(HEADS, r.tile_small, r.small_hd)
    r.units_in[pl.ds(s, 1)] = r.w_in[...][None]
    r.units_out[pl.ds(s, 1)] = r.w_out[...][None]
    finish(copies)
    x_copies = sender.share(CTX, r.tokens_in.at[s], groups[FWD][ALL_X])
    copies = sender.push(HEADS, lambda p: r.tile_in, lambda me: r.w_qkv.at[s, :, me])
    copies += sender.push(CTX, lambda p: r.small_hd, lambda me: r.small_all.at[s, me])
    finish(copies)
    copies = []
    for ref in (r.w_qkv, r.w_mix, r.small_all):
        copies += sender.push(
            SECTION, lambda p, a=ref: a.at[s], lambda me, a=ref: a.at[me], keep=False
        )
    finish(copies)

    lanes = r.tile_small.shape[1]
    spread_rows = lax.broadcasted_iota(jnp.int32, (lanes, width), 0)
    spread_cols = lax.broadcasted_iota(jnp.int32, (lanes, width), 1)
    length2 = r.buckets.shape[1]
    bias_lane = lax.broadcasted_iota(jnp.int32, (lanes, length2), 0)
    bias_share = r.diag_marks.shape[0] * heads // hd_count
    bucket_count = r.diag_marks.shape[0]
    for layer in range(2):
        total = jnp.zeros((r.tile_small.shape[0], width), jnp.float32)
        for i in range(ctx_count):
            for j in range(hd_count):
                at = (i * hd_count + j) * share
                hit = (spread_rows + at == spread_cols) & (spread_rows < share)
                total = total + dot_f32(r.small_all[layer, i, j], low(jnp.where(hit, 1.0, 0.0)))
        r.small[layer] = total
        r.bias[layer] = jnp.zeros(r.bias.shape[1:], jnp.float32)
        for head in range(heads):
            row = jnp.zeros((r.tile_small.shape[0], length2), jnp.float32)
            for j in range(hd_count):
                hit = (bias_lane + (j * bias_share - head * bucket_count) == r.buckets[...]) & (
                    bias_lane < bias_share
                )
                row = row + dot_f32(
                    r.small_all[layer, pl.ds(c, 1), j][0], low(jnp.where(hit, 1.0, 0.0))
                )
            r.bias[layer, head : head + 1] = row[2 + experts : 3 + experts]

    late = []

    def put_for(layer):
        def put(entering, value):
            kept, sent = (r.g_in, r.g_in_low) if entering else (r.g_out, r.g_out_low)

            @pl.when(s == layer)
            def _():
                kept[...] = value

            @pl.when(s != layer)
            def _():
                sent[...] = low(value)

        return put

    def units_done():
        late.extend(sender.push(SECTION, lambda p: r.g_in_low, lambda me: r.g_in_got, keep=False))
        late.extend(sender.push(SECTION, lambda p: r.g_out_low, lambda me: r.g_out_got, keep=False))
        late.extend(
            sender.push(
                SECTION, lambda p: r.made.at[other], lambda me: r.section_out.at[me], keep=False
            )
        )
        r.section_out[pl.ds(s, 1)] = r.made[pl.ds(s, 1)]

    def view(mode, layer, x):
        refs = dict(groups[mode])
        if mode == BACK:
            refs.update((name, groups[FWD][name]) for name in SAVED)
        refs.update(routed=groups[BOTH if mode == BOTH else FWD][GATHERED])
        refs.update(
            x=x,
            small=r.small.at[layer],
            bias=r.bias.at[layer],
            route=r.route.at[layer],
            w_qkv=r.w_qkv.at[layer],
            w_mix=r.w_mix.at[layer],
            w_in=r.units_in.at[layer],
            w_out=r.units_out.at[layer],
            experts=experts,
            x_copies=x_copies if mode == FWD else None,
            produced=r.made.at[layer],
            grad_in=r.made_grad.at[layer],
            g_qkv=r.g_qkv_all.at[layer],
            g_mix=r.g_mix_all.at[layer],
            g_small=r.g_small_all.at[layer],
            put=put_for(layer),
            before_experts=(lambda: finish(unit_copies)) if mode == FWD else (lambda: None),
            after_units=units_done if mode == BACK else (lambda: None),
        )
        return types.SimpleNamespace(**refs)

    tokens = r.tokens_in.at[s]
    first = view(FWD, 0, tokens)
    layer_pass(FWD, heads, sender, first)
    second = view(BOTH, 1, r.made.at[0])
    second.cot = r.grad_out.at[s]
    layer_pass(BOTH, heads, sender, second)
    back = view(BACK, 0, tokens)
    back.cot = r.made_grad.at[1]
    layer_pass(BACK, heads, sender, back)

    for layer, refs in ((0, back), (1, second)):
        r.g_bias_all[layer] = lax.dot_general(
            refs.diag[...],
            r.diag_marks[...],
            COLS_IN,
            precision=highest,
            preferred_element_type=jnp.float32,
        )
    r.g_qkv_low[...] = low(r.g_qkv_all[pl.ds(other, 1)][0])
    r.g_mix_low[...] = low(r.g_mix_all[pl.ds(other, 1)][0])
    copies = []
    for source, target in (
        (r.g_qkv_low, r.g_qkv_got),
        (r.g_mix_low, r.g_mix_got),
        (r.g_small_all.at[other], r.g_small_got),
        (r.g_bias_all.at[other], r.g_bias_got),
    ):
        copies += sender.push(SECTION, lambda p, a=source: a, lambda me, b=target: b, keep=False)
    late.extend(
        sender.push(
            SECTION, lambda p: r.made_grad.at[other], lambda me: r.in_grad.at[me], keep=False
        )
    )
    r.in_grad[pl.ds(s, 1)] = r.made_grad[pl.ds(s, 1)]
    finish(copies)
    qkv_sum = r.g_qkv_all[pl.ds(s, 1)][0] + r.g_qkv_got[...].astype(jnp.float32)
    mix_sum = r.g_mix_all[pl.ds(s, 1)][0] + r.g_mix_got[...].astype(jnp.float32)
    r.small_one[...] = r.g_small_all[pl.ds(s, 1)][0] + r.g_small_got[...]
    r.bias_one[...] = r.g_bias_all[pl.ds(s, 1)][0] + r.g_bias_got[...]
    for i in range(ctx_count):
        for j in range(hd_count):
            at = (i * hd_count + j) * share
            r.qkv_out[j, i] = low(qkv_sum[at : at + share])
    for j in range(hd_count):
        r.mix_grad_out[j] = low(mix_sum[j * share : (j + 1) * share])
    copies = sender.spread(HEADS, r.qkv_out, r.qkv_in)
    copies += sender.spread(HEADS, r.mix_grad_out, r.mix_grad_in)
    copies += sender.share(HEADS, r.small_one, r.small_one_in)
    copies += sender.share(HEADS, r.bias_one, r.bias_one_in)
    finish(copies)
    r.g_output[...] = sum_tiles(r.mix_grad_in)
    r.g_bias[...] = sum_tiles(r.bias_one_in)
    r.small_two[...] = sum_tiles(r.small_one_in)
    for i in range(ctx_count):
        total = r.qkv_in[0, i].astype(jnp.float32)
        for j in range(1, hd_count):
            total = total + r.qkv_in[j, i].astype(jnp.float32)
        r.cols_out[i] = low(total)
    copies = sender.spread(CTX, r.cols_out, r.cols_in)
    copies += sender.share(CTX, r.small_two, r.small_two_in)
    finish(late)
    r.g_in[...] += r.g_in_got[...].astype(jnp.float32)
    r.g_out[...] += r.g_out_got[...].astype(jnp.float32)
    finish(copies)
    r.g_small[...] = sum_tiles(r.small_two_in)
    for at, ref in enumerate((r.g_query, r.g_key, r.g_value)):
        for i in range(ctx_count):
            ref[:, i * group : (i + 1) * group] = r.cols_in[
                i, :, at * group : (at + 1) * group
            ].astype(jnp.float32)


def step_call(heads, experts, ctx_count, hd_count, operands):
    rows, width = operands.tokens_in.shape[1:]
    share = operands.w_query.shape[0]
    units = operands.w_in.shape[1]
    length, group = rows * ctx_count, heads * HD
    capacity = max(2, 2 * rows // experts)
    slots = experts * capacity
    total = slots * hd_count
    small_rows = operands.tile_small.shape[0]
    buckets = operands.diag_marks.shape[0]
    head_rows = heads + -heads % 8
    g_rows = 2 + experts + -(2 + experts) % 8
    b16, f32, i32 = jnp.bfloat16, jnp.float32, jnp.int32
    outs = dict(
        section_out=((2, rows, width), b16),
        in_grad=((2, rows, width), b16),
        g_query=((share, width), f32),
        g_key=((share, width), f32),
        g_value=((share, width), f32),
        g_output=((share, width), f32),
        g_small=((g_rows, width), f32),
        g_bias=((head_rows, buckets), f32),
        g_in=((width, units), f32),
        g_out=((units, width), f32),
    )
    scratch = dict(
        units_in=((2, width, units), b16),
        units_out=((2, units, width), b16),
        tile_out=((ctx_count, share, 3 * group), b16),
        tile_in=((ctx_count, share, 3 * group), b16),
        route=((2, rows, 1), i32),
        w_mix=((2, hd_count, share, width), b16),
        w_qkv=((2, ctx_count, hd_count, share, 3 * group), b16),
        small_hd=((hd_count, small_rows, operands.tile_small.shape[1]), b16),
        small_all=((2, ctx_count, hd_count, small_rows, operands.tile_small.shape[1]), b16),
        small=((2, small_rows, width), f32),
        bias=((2, head_rows, 2 * length), f32),
        made=((2, rows, width), b16),
        made_grad=((2, rows, width), b16),
        g_qkv_all=((2, width, 3 * group), f32),
        g_mix_all=((2, group, width), f32),
        g_small_all=((2, g_rows, width), f32),
        g_bias_all=((2, head_rows, buckets), f32),
        g_in_low=((width, units), b16),
        g_in_got=((width, units), b16),
        g_out_low=((units, width), b16),
        g_out_got=((units, width), b16),
        g_qkv_low=((width, 3 * group), b16),
        g_qkv_got=((width, 3 * group), b16),
        g_mix_low=((group, width), b16),
        g_mix_got=((group, width), b16),
        g_small_got=((g_rows, width), f32),
        g_bias_got=((head_rows, buckets), f32),
        small_one=((g_rows, width), f32),
        small_one_in=((hd_count, g_rows, width), f32),
        small_two=((g_rows, width), f32),
        small_two_in=((ctx_count, g_rows, width), f32),
        bias_one=((head_rows, buckets), f32),
        bias_one_in=((hd_count, head_rows, buckets), f32),
        qkv_out=((hd_count, ctx_count, share, 3 * group), b16),
        qkv_in=((hd_count, ctx_count, share, 3 * group), b16),
        mix_grad_out=((hd_count, share, width), b16),
        mix_grad_in=((hd_count, share, width), b16),
        cols_out=((ctx_count, share, 3 * group), b16),
        cols_in=((ctx_count, share, 3 * group), b16),
    )
    saved = dict(
        normed=((length, width), b16),
        qkv=((length, 3 * group), b16),
        attended=((length, group), b16),
        mid=((rows, width), f32),
        two=((rows, width), b16),
        probs=((rows, experts), f32),
        gate=((rows, 1), f32),
        disp=((rows, slots), b16),
        hidden=((ctx_count, total // ctx_count, units), f32),
        result=((rows, width), f32),
    )
    for mode in (FWD, BOTH, BACK):
        wide = 2 * width if mode == BOTH else width
        own = dict(
            slot_out=((ctx_count, capacity, wide), b16),
            slot_in=((ctx_count, capacity, wide), b16),
                        gathered=((ctx_count, hd_count, capacity, wide), b16),
            term_out=((ctx_count, hd_count, capacity, wide), b16),
            term_in=((ctx_count, hd_count, capacity, wide), b16),
            back_out=((ctx_count, capacity, wide), b16),
            back_in=((ctx_count, capacity, wide), b16),
        )
        if mode != BACK:
            own.update(saved)
            tiles = ((ctx_count, rows, width), b16)
            own.update(all_x=tiles, mix_out=tiles, mix_in=tiles)
        if mode != FWD:
            own.update(active=((ctx_count, total // ctx_count, units), b16))
            own.update(grad_hidden=((ctx_count, total // ctx_count, units), b16))
            own.update(mid_out=((rows, width), b16))
            own.update(diag=((head_rows, 2 * length), f32))
            tiles = ((ctx_count, rows, width), b16)
            own.update(mid_in=tiles, norm_out=tiles, norm_in=tiles)
        for name, shape in own.items():
            scratch[mode, name] = shape
    flat = vars(operands)
    names = [(0, name) for name in (*flat, *outs)]
    names += [(0, name) if isinstance(name, str) else name for name in scratch]
    results = pl.pallas_call(
        functools.partial(step_kernel, heads, experts, names),
        out_shape=[jax.ShapeDtypeStruct(*shape) for shape in outs.values()],
        in_specs=[pl.BlockSpec(memory_space=pltpu.VMEM)] * len(flat),
        out_specs=[pl.BlockSpec(memory_space=pltpu.VMEM)] * len(outs),
        scratch_shapes=[pltpu.VMEM(*shape) for shape in scratch.values()]
        + [pltpu.SemaphoreType.DMA((SEMAPHORES, 2))],
        compiler_params=pltpu.CompilerParams(
            collective_id=0, has_side_effects=True, vmem_limit_bytes=60 * 2**20
        ),
    )(*flat.values())
    return types.SimpleNamespace(**dict(zip(outs, results)))


SEMAPHORES = 176


def on_device_heads(
    tokens_in,
    grad_out,
    w_query,
    w_key,
    w_value,
    w_output,
    gain_attn,
    gain_ffn,
    router,
    rel_bias,
    w_in,
    w_out,
    routes,
    relative_bucket,
):
    ctx_count, hd_count = lax.axis_size(CTX), lax.axis_size(HEADS)
    share = w_query.shape[1]
    heads = H // ctx_count
    experts = router.shape[2]
    length = (relative_bucket.shape[0] + 1) // 2
    bias_share = rel_bias.shape[1]
    bucket_count = bias_share * ctx_count * hd_count // H
    lanes = share + -share % 128
    pad_rows = -(3 + experts) % 16
    bias_row = jnp.pad(rel_bias, ((0, 0), (0, share - bias_share)))
    tile_small = jnp.concatenate([gain_attn, gain_ffn, router[0].T, bias_row], axis=0)
    tile_small = jnp.pad(tile_small, ((0, pad_rows), (0, lanes - share)))
    buckets = jnp.concatenate(
        [relative_bucket[:length][::-1], relative_bucket[:1], relative_bucket[length:][::-1]]
    )[None]
    diag_buckets = jnp.concatenate([relative_bucket[::-1], relative_bucket[:1] * 0 - 1])
    diag_marks = (
        jnp.arange(bucket_count, dtype=jnp.int32)[:, None] == diag_buckets[None]
    ).astype(jnp.float32)
    grads = step_call(
        heads,
        experts,
        ctx_count,
        hd_count,
        types.SimpleNamespace(
            tokens_in=tokens_in,
            grad_out=grad_out,
            w_query=w_query[0],
            w_key=w_key[0],
            w_value=w_value[0],
            w_output=w_output[0],
            tile_small=tile_small,
            w_in=w_in[0, 0],
            w_out=w_out[0, 0],
            routes=routes[0],
            buckets=buckets,
            diag_marks=diag_marks,
        ),
    )
    place = lax.axis_index(CTX) * hd_count + lax.axis_index(HEADS)
    small = lax.dynamic_slice_in_dim(grads.g_small, place * share, share, 1)
    bias = lax.dynamic_slice_in_dim(
        grads.g_bias[:heads].reshape(-1), lax.axis_index(HEADS) * bias_share, bias_share, 0
    )
    return (
        grads.section_out[None],
        grads.in_grad[None],
        grads.g_query[None],
        grads.g_key[None],
        grads.g_value[None],
        grads.g_output[None],
        small[0:1],
        small[1:2],
        small[2 : 2 + experts].T[None],
        bias[None],
        grads.g_in[None, None],
        grads.g_out[None, None],
    )


def solution(mesh):
    in_specs = (
        P(None, (CTX, HEADS), None),
        P(None, (CTX, HEADS), None),
        P(SECTION, (CTX, HEADS), None),
        P(SECTION, (CTX, HEADS), None),
        P(SECTION, (CTX, HEADS), None),
        P(SECTION, (CTX, HEADS), None),
        P(SECTION, (CTX, HEADS)),
        P(SECTION, (CTX, HEADS)),
        P(SECTION, (CTX, HEADS), None),
        P(SECTION, (CTX, HEADS)),
        P(SECTION, CTX, None, HEADS),
        P(SECTION, CTX, HEADS, None),
        P(SECTION, None, (CTX, HEADS), None),
        P(),
    )
    out_specs = (
        P(SECTION, None, (CTX, HEADS), None),
        P(SECTION, None, (CTX, HEADS), None),
        P(SECTION, (CTX, HEADS), None),
        P(SECTION, (CTX, HEADS), None),
        P(SECTION, (CTX, HEADS), None),
        P(SECTION, (CTX, HEADS), None),
        P(SECTION, (CTX, HEADS)),
        P(SECTION, (CTX, HEADS)),
        P(SECTION, (CTX, HEADS), None),
        P(SECTION, (CTX, HEADS)),
        P(SECTION, CTX, None, HEADS),
        P(SECTION, CTX, HEADS, None),
    )
    by_heads = H % mesh.shape[CTX] == 0
    return jax.shard_map(
        on_device_heads if by_heads else on_device, mesh=mesh, in_specs=in_specs, out_specs=out_specs, check_vma=False
    )
```
